256 devices in a mesh: rep: 2 (over z_hi), ctx: 128 (over x, y, z_lo, core).
Axes of the slice: x: 4, y: 4, z: 8 (z_hi: 2, z_lo: 4; z = z_hi * 4 + z_lo), core: 2. Of those that a mesh axis runs over, the one named last changes fastest.
Arguments:
- inputs: bfloat16 [2, 16384, 4096], P('rep', 'ctx'), may hold values from -6 to 6
- gate_li: bfloat16 [2, 16384, 4096], P('rep', 'ctx'), may hold values from -6 to 6
- gate_mr: bfloat16 [2, 16384, 4096], P('rep', 'ctx'), may hold values from -6 to 6
- cotangent: bfloat16 [2, 16384, 4096], P('rep', 'ctx'), may hold values from -6 to 6
- residues: float32 [128, 16], replicated, may hold values from -1.5 to 1.5
- rates: float32 [128, 16], replicated, may hold values from 1.2207031e-05 to 0.05
- taps: float32 [128, 128], replicated, may hold values from -0.5 to 0.5
Outputs:
- grad_inputs: bfloat16 [2, 16384, 4096], P('rep', 'ctx')
- grad_gate_li: bfloat16 [2, 16384, 4096], P('rep', 'ctx')
- grad_gate_mr: bfloat16 [2, 16384, 4096], P('rep', 'ctx')
- grad_residues: float32 [128, 16], replicated
- grad_taps: float32 [128, 128], replicated
The draws below stay inside these ranges and needn't reach their ends.
All inputs are finite; a program needn't handle non-finite values.
Results may differ from the reference program's by a relative error of at most 0.0049.
Values may be sent and summed in bfloat16 or wider, within the bound.
No kernel may reach another device: no remote copies, remote signals or barrier semaphores. Data moves between devices by JAX's collectives and lax.ppermute only.
A program may use at most 320 MiB of HBM per device.

```python
import math
import jax
import jax.numpy as jnp
from jax import lax

D = 4096
GROUP = 32
MODES = 16
TAPS = 128
G = 128
NPOS = 16384
N_REP = 2


def block_levels(stream_key, shape, split, smallest, top_value):
    loudness = 1.0
    for dim, blocks in split:
        heights = jax.random.uniform(jax.random.fold_in(jax.random.fold_in(stream_key, 6), dim), (blocks,), jnp.float32, smallest / len(split), top_value / len(split))
        loudness = loudness * jnp.repeat(jnp.exp(heights), shape[dim] // blocks).reshape((-1,) + (1,) * (len(shape) - 1 - dim))
    return loudness


def centred(key, shape, deviation, most, pieces=(), kind=jnp.bfloat16):
    drawn = jax.random.normal(key, shape, jnp.float32) * deviation
    if len(pieces) > 0:
        drawn = block_levels(key, shape, pieces, -0.22, 0.18) * drawn
    return jnp.clip(drawn, min=-most, max=most).astype(kind)


def setup_inputs(seed: int = 0) -> dict:
    seeds = jax.random.split(jax.random.key(seed), 8)
    return {
        "inputs": centred(seeds[0], (N_REP, NPOS, D), 1.0, 6.0, ((0, 2), (1, 128))),
        "gate_li": centred(seeds[1], (N_REP, NPOS, D), 1.0, 6.0, ((0, 2), (1, 128))),
        "gate_mr": centred(seeds[2], (N_REP, NPOS, D), 1.0, 6.0, ((0, 2), (1, 128))),
        "cotangent": centred(seeds[3], (N_REP, NPOS, D), 1.0, 6.0, ((0, 2), (1, 128))),
        "residues": centred(seeds[4], (G, MODES), MODES ** -0.5, 1.5, (), jnp.float32),
        "rates": jnp.clip(jnp.exp(jax.random.uniform(seeds[5], (G, MODES), jnp.float32, math.log(1.220703143189894e-05), math.log(0.05))), 1.220703143189894e-05, 0.05),
        "taps": centred(seeds[6], (G, TAPS), TAPS ** -0.5, 0.5, (), jnp.float32),
    }


def causal_fft(signal, kernel):
    length = signal.shape[1]
    padded_len = 2 * length
    spectrum = jnp.fft.rfft(signal, n=padded_len, axis=1) * jnp.fft.rfft(kernel, n=padded_len)[None, :, None]
    return jnp.fft.irfft(spectrum, n=padded_len, axis=1)[:, :length].astype(signal.dtype)

def anticausal_fft(signal, kernel):
    return jnp.flip(causal_fft(jnp.flip(signal, 1), kernel), 1)

def lag_sums(later_seq, earlier_seq, count):
    padded_len = 2 * later_seq.shape[1]
    spectrum = jnp.fft.rfft(later_seq, n=padded_len, axis=1) * jnp.conj(jnp.fft.rfft(earlier_seq, n=padded_len, axis=1))
    spectrum = lax.optimization_barrier(jnp.sum(spectrum, axis=(0, 2)))
    return jnp.fft.irfft(spectrum, n=padded_len)[:count].astype(later_seq.dtype)

def reference(inputs, gate_li, gate_mr, cotangent, residues, rates, taps):
    length = inputs.shape[1]
    lag_steps = jnp.arange(length).astype(jnp.float32)
    norm_factor = jnp.sqrt(-jnp.expm1(-2.0 * rates))

    def per_group(group_index):

        def cut(array):
            return lax.dynamic_slice_in_dim(array, group_index * GROUP, GROUP, 2).astype(jnp.float32)
        rate_row = lax.dynamic_index_in_dim(rates, group_index, 0, keepdims=False)
        resid_row = lax.dynamic_index_in_dim(residues, group_index, 0, keepdims=False)
        norm_row = lax.dynamic_index_in_dim(norm_factor, group_index, 0, keepdims=False)
        tap_row = lax.dynamic_index_in_dim(taps, group_index, 0, keepdims=False)
        powers = jnp.exp(-rate_row[:, None] * lag_steps[None, :])
        li_filter = lax.optimization_barrier(jnp.sum((resid_row * norm_row)[:, None] * powers, axis=0))
        mr_filter = jnp.pad(tap_row, (0, length - TAPS))
        seq_in = cut(inputs)
        gate_one = cut(gate_li)
        gate_two = cut(gate_mr)
        cot_out = cut(cotangent)
        li_values = causal_fft(seq_in, li_filter)
        mixer_in = (gate_one * li_values).astype(jnp.bfloat16).astype(jnp.float32)
        mixed_out = causal_fft(mixer_in, mr_filter)
        grad_gate_mr = (cot_out * mixed_out).astype(jnp.bfloat16)
        scaled = (cot_out * gate_two).astype(jnp.bfloat16).astype(jnp.float32)
        grad_mixer = anticausal_fft(scaled, mr_filter)
        tap_sums = lag_sums(scaled, mixer_in, TAPS)
        grad_gate_li = (grad_mixer * li_values).astype(jnp.bfloat16)
        cot_li = grad_mixer * gate_one
        grad_inputs = anticausal_fft(cot_li, li_filter).astype(jnp.bfloat16)
        correlation = lag_sums(cot_li, seq_in, length)
        residue_sums = norm_row * lax.optimization_barrier(jnp.sum(powers * correlation[None, :], axis=1))
        return (grad_inputs, grad_gate_li, grad_gate_mr, residue_sums, tap_sums)
    results = lax.map(per_group, jnp.arange(G).astype(jnp.int32))

    def unfold(stacked):
        return jnp.transpose(stacked, (1, 2, 0, 3)).reshape(N_REP, length, D)
    grad_scale = 1.0 / math.sqrt(N_REP * length)
    return (unfold(results[0]), unfold(results[1]), unfold(results[2]), results[3] * grad_scale, results[4] * grad_scale)
```

```python
import functools
import math

import jax
import jax.numpy as jnp
from jax import lax
from jax.experimental import pallas as pl
from jax.experimental.pallas import tpu as pltpu
from jax.sharding import PartitionSpec as P

F32 = jnp.float32
BF16 = jnp.bfloat16
LANES = 128
NN = (((1,), (0,)), ((), ()))
NT = (((1,), (1,)), ((), ()))
TN = (((0,), (0,)), ((), ()))
VMEM_LIMIT = 48 * 1024 * 1024


def dot(left, right, dims=NN):
    return lax.dot_general(left, right, dims, preferred_element_type=F32)


def split(x):
    high = x.astype(BF16)
    return high, (x - high.astype(F32)).astype(BF16)


def iota(shape, dim):
    return lax.broadcasted_iota(jnp.int32, shape, dim)


def roll_left(x, amount):
    return pltpu.roll(x, x.shape[1] - amount, 1)


def pick_groups(stacked, rows, size):
    lane_group = iota((rows, LANES), 1) // size
    out = stacked[:rows]
    for g in range(1, LANES // size):
        out = jnp.where(lane_group == g, stacked[g * rows : (g + 1) * rows], out)
    return out


def spread_groups(x, size):
    lane_group = iota(x.shape, 1) // size
    zero = jnp.zeros_like(x)
    return jnp.concatenate(
        [jnp.where(lane_group == g, x, zero) for g in range(LANES // size)], axis=0
    )


def circulant(row):
    return pltpu.roll(jnp.broadcast_to(row, (LANES, LANES)), 0, 1, stride=1, stride_axis=0)


def lag_sum(z):
    rows = LANES
    while rows > 8:
        rows //= 2
        z = z[:rows] + roll_left(z[rows:], rows)
    sub = iota((8, LANES), 0)
    for bit in (4, 2, 1):
        z = jnp.where((sub & bit) != 0, roll_left(z, bit), z)
    return jnp.sum(z, axis=0, keepdims=True)


def carried_part(table, entering, size):
    t_high, t_low = split(table)
    e_high, e_low = split(entering)
    e_high, e_low = spread_groups(e_high, size), spread_groups(e_low, size)
    return dot(
        jnp.concatenate([t_high, t_high, t_low], axis=0),
        jnp.concatenate([e_high, e_low, e_high], axis=0),
        TN,
    )


def states_kernel(size, modes, x_ref, table_ref, out_ref):
    per = LANES // size
    for i in range(x_ref.shape[1] // LANES):
        lanes = slice(i * LANES, (i + 1) * LANES)
        high, low = split(table_ref[i * per * modes : (i + 1) * per * modes, :])
        prod = dot(jnp.concatenate([high, low], axis=0), x_ref[:, lanes])
        prod = prod[: per * modes] + prod[per * modes :]
        out_ref[i * modes : (i + 1) * modes, :] = pick_groups(prod, modes, size)


def mixer_back_kernel(
    size, modes, own_ref, next_ref, gate_ref, x_ref, taps_ref, table_ref, gm_ref, out_ref, lag_ref
):
    per = LANES // size
    row, col = iota((LANES, LANES), 0), iota((LANES, LANES), 1)
    for i in range(x_ref.shape[1] // LANES):
        lanes = slice(i * LANES, (i + 1) * LANES)
        mats = []
        for g in range(per):
            full = circulant(taps_ref[i * per + g : i * per + g + 1, :])
            high, low = split(full)
            zero = jnp.zeros_like(high)
            mats.append(
                jnp.concatenate(
                    [jnp.where(col >= row, high, zero), jnp.where(col < row, high, zero),
                     jnp.where(col >= row, low, zero), jnp.where(col < row, low, zero)],
                    axis=1,
                )
            )
        own, after = own_ref[:, lanes], next_ref[:, lanes]
        prod = dot(jnp.concatenate(mats, axis=0), jnp.concatenate([own, after, own, after], axis=0))
        grad_mixer = pick_groups(prod, LANES, size)
        gm_ref[:, lanes] = grad_mixer
        cot = grad_mixer * gate_ref[:, lanes].astype(F32)
        high, low = split(cot)
        t_high, t_low = split(table_ref[i * per * modes : (i + 1) * per * modes, :])
        left = jnp.concatenate(
            [jnp.concatenate([t_high, t_high], axis=1), jnp.concatenate([t_low, t_low], axis=1)], axis=0
        )
        prod = dot(left, jnp.concatenate([high, low], axis=0))
        prod = prod[: per * modes] + prod[per * modes :]
        out_ref[i * modes : (i + 1) * modes, :] = pick_groups(prod, modes, size)
        pairs = dot(spread_groups(x_ref[:, lanes], size), high, NT)
        for g in range(per):
            z = jnp.where(col >= row, pairs[g * LANES : (g + 1) * LANES], 0.0)
            lag_ref[i * per + g : i * per + g + 1, :] = lag_sum(z)


def values_kernel(
    size, modes, x_ref, gate_ref, gm_ref, own_ref, next_ref, filt_ref, table_ref, enter_ref,
    mix_ref, ggl_ref, lag_ref,
):
    per = LANES // size
    row, col = iota((LANES, LANES), 0), iota((LANES, LANES), 1)
    for i in range(x_ref.shape[1] // LANES):
        lanes = slice(i * LANES, (i + 1) * LANES)
        mats = []
        for g in range(per):
            full = circulant(filt_ref[i * per + g : i * per + g + 1, :])
            high, low = split(jnp.where(col <= row, full, 0.0))
            mats.append(jnp.concatenate([high, low], axis=1))
        x = x_ref[:, lanes]
        prod = dot(jnp.concatenate(mats, axis=0), jnp.concatenate([x, x], axis=0))
        values = pick_groups(prod, LANES, size) + carried_part(
            table_ref[i * per * modes : (i + 1) * per * modes, :],
            enter_ref[i * modes : (i + 1) * modes, :],
            size,
        )
        ggl_ref[:, lanes] = (gm_ref[:, lanes] * values).astype(BF16)
        mix = (gate_ref[:, lanes].astype(F32) * values).astype(BF16)
        mix_ref[:, lanes] = mix
        both = jnp.concatenate([own_ref[:, lanes], next_ref[:, lanes]], axis=0)
        pairs = dot(spread_groups(mix, size), both, NT)
        for g in range(per):
            z = pairs[g * LANES : (g + 1) * LANES]
            lag_ref[i * per + g : i * per + g + 1, :] = lag_sum(
                jnp.where(col >= row, z[:, :LANES], z[:, LANES:])
            )


def input_grad_kernel(size, modes, gm_ref, gate_ref, filt_ref, table_ref, enter_ref, out_ref):
    per = LANES // size
    row, col = iota((LANES, LANES), 0), iota((LANES, LANES), 1)
    for i in range(gm_ref.shape[1] // LANES):
        lanes = slice(i * LANES, (i + 1) * LANES)
        mats = []
        for g in range(per):
            full = circulant(filt_ref[i * per + g : i * per + g + 1, :])
            high, low = split(jnp.where(col >= row, full, 0.0))
            mats.append(jnp.concatenate([high, low, high], axis=1))
        high, low = split(gm_ref[:, lanes] * gate_ref[:, lanes].astype(F32))
        prod = dot(jnp.concatenate(mats, axis=0), jnp.concatenate([high, high, low], axis=0))
        out_ref[:, lanes] = (
            pick_groups(prod, LANES, size)
            + carried_part(
                table_ref[i * per * modes : (i + 1) * per * modes, :],
                enter_ref[i * modes : (i + 1) * modes, :],
                size,
            )
        ).astype(BF16)


def mixer_kernel(size, own_ref, before_ref, taps_ref, cot_ref, out_ref):
    per = LANES // size
    row, col = iota((LANES, LANES), 0), iota((LANES, LANES), 1)
    for i in range(own_ref.shape[1] // LANES):
        lanes = slice(i * LANES, (i + 1) * LANES)
        mats = []
        for g in range(per):
            high, low = split(circulant(taps_ref[i * per + g : i * per + g + 1, :]))
            zero = jnp.zeros_like(high)
            mats.append(
                jnp.concatenate(
                    [jnp.where(col <= row, high, zero), jnp.where(col > row, high, zero),
                     jnp.where(col <= row, low, zero), jnp.where(col > row, low, zero)],
                    axis=1,
                )
            )
        own, before = own_ref[:, lanes], before_ref[:, lanes]
        prod = dot(jnp.concatenate(mats, axis=0), jnp.concatenate([own, before, own, before], axis=0))
        mixed = pick_groups(prod, LANES, size)
        out_ref[:, lanes] = (cot_ref[:, lanes].astype(F32) * mixed).astype(BF16)


def scan_kernel(x_ref, decay_ref, out_ref):
    decay = decay_ref[...]
    state = jnp.zeros_like(decay)
    for d in range(x_ref.shape[0]):
        out_ref[d] = state
        state = decay * state + x_ref[d]


def back_scan_kernel(rows, x_ref, decay_ref, front_ref, out_ref, sum_ref):
    decay = decay_ref[...]
    state = jnp.zeros_like(decay)
    total = jnp.zeros_like(decay)
    for d in reversed(range(x_ref.shape[0])):
        x = x_ref[d, rows:, :]
        out_ref[d] = state
        state = decay * state + x
        total = total + x * front_ref[d]
    sum_ref[...] = total


def call(body, width, step, specs, outs, args, flops):
    def block(rows):
        if rows is None:
            return pl.BlockSpec((LANES, step), lambda i: (0, i))
        return pl.BlockSpec((rows, LANES), lambda i: (i, 0))

    def shape(rows, kind):
        if rows is None:
            return jax.ShapeDtypeStruct((LANES, width), kind)
        return jax.ShapeDtypeStruct((rows * (width // step), LANES), kind)

    nbytes = sum(a.size * a.dtype.itemsize for a in args)
    return pl.pallas_call(
        body,
        grid=(width // step,),
        in_specs=[block(rows) for rows in specs],
        out_specs=[block(rows) for rows, kind in outs],
        out_shape=[shape(rows, kind) for rows, kind in outs],
        compiler_params=pltpu.CompilerParams(vmem_limit_bytes=VMEM_LIMIT),
        cost_estimate=pl.CostEstimate(flops=flops, bytes_accessed=nbytes, transcendentals=0),
    )(*args)


def whole(body, outs, args):
    return pl.pallas_call(
        body,
        out_shape=[jax.ShapeDtypeStruct(s, F32) for s in outs],
        compiler_params=pltpu.CompilerParams(vmem_limit_bytes=VMEM_LIMIT),
    )(*args)


def shifted(x, by):
    count = lax.axis_size("ctx")
    return lax.ppermute(x, "ctx", [(i, i + by) for i in range(count) if 0 <= i + by < count])


def exchange(x, axes="ctx"):
    return lax.all_to_all(x, axes, split_axis=0, concat_axis=0, tiled=True)


def on_device(inputs, gate_li, gate_mr, cotangent, residues, rates, taps):
    seq, gate, cot = inputs[0], gate_li[0], cotangent[0]
    width = seq.shape[1]
    groups, modes = rates.shape
    size = width // groups
    per = LANES // size
    tiles = width // LANES
    reps, count = lax.axis_size("rep"), lax.axis_size("ctx")
    me = lax.axis_index("ctx")
    own_rows = tiles * modes // count
    step = min(512, width)
    state_rows = step // LANES * modes
    table_rows = per * state_rows
    group_rows = step // size

    scaled = (cot.astype(F32) * gate_mr[0].astype(F32)).astype(BF16)
    after = shifted(scaled, -1)

    lags = jnp.arange(LANES).astype(F32)
    norm = jnp.sqrt(-jnp.expm1(-2.0 * rates))
    weight = residues * norm
    rate3, weight3 = rates[:, :, None], weight[:, :, None]
    lam = jnp.exp(-rate3 * lags)
    filt = jnp.sum(weight3 * lam, axis=1)
    filt_back = jnp.roll(jnp.flip(filt, 1), 1, axis=1)
    taps_back = jnp.roll(jnp.flip(taps, 1), 1, axis=1)
    to_end = jnp.exp(-rate3 * (LANES - 1.0 - lags))
    from_start = jnp.exp(-rate3 * (lags + 1.0))
    flat = (groups * modes, LANES)
    end_table = to_end.reshape(flat)
    start_table = from_start.reshape(flat)
    front_table = (weight3 * from_start).reshape(flat)
    back_table = (weight3 * to_end).reshape(flat)
    decay = jnp.exp(-rates * LANES).reshape(tiles, per, modes)
    decay = jnp.repeat(jnp.swapaxes(decay, 1, 2).reshape(tiles * modes, per), size, axis=1)
    decay = lax.dynamic_slice_in_dim(decay, me * own_rows, own_rows, 0)

    bind = functools.partial
    states = call(
        bind(states_kernel, size, modes), width, step, [None, table_rows], [(state_rows, F32)],
        [seq, end_table], 2 * LANES * width * 64,
    )[0]
    ends = exchange(states.reshape(count, own_rows, LANES))
    entering = whole(scan_kernel, [ends.shape], [ends, decay])[0]

    grad_mixer, back_states, lag_cot = call(
        bind(mixer_back_kernel, size, modes), width, step,
        [None, None, None, None, group_rows, table_rows],
        [(None, F32), (state_rows, F32), (group_rows, F32)],
        [scaled, after, gate, seq, taps, start_table], 2 * LANES * width * 1024,
    )
    second = exchange(
        jnp.concatenate([entering, back_states.reshape(count, own_rows, LANES)], axis=1)
    )
    back_entering, state_sums = whole(
        bind(back_scan_kernel, own_rows), [ends.shape, decay.shape], [second, decay, entering]
    )

    mixer_in, grad_gate_li, lag_taps = call(
        bind(values_kernel, size, modes), width, step,
        [None, None, None, None, None, group_rows, table_rows, state_rows],
        [(None, BF16), (None, BF16), (group_rows, F32)],
        [seq, gate, grad_mixer, scaled, after, filt_back, front_table,
         second[:, :own_rows].reshape(tiles * modes, LANES)], 2 * LANES * width * 1024,
    )
    before = shifted(mixer_in, 1)
    third = exchange(
        jnp.concatenate(
            [back_entering, lag_taps.reshape(count, -1, LANES), lag_cot.reshape(count, -1, LANES)], axis=1
        )
    )
    own_groups = groups // count
    grad_inputs = call(
        bind(input_grad_kernel, size, modes), width, step,
        [None, None, group_rows, table_rows, state_rows], [(None, BF16)],
        [grad_mixer, gate, filt, back_table, third[:, :own_rows].reshape(tiles * modes, LANES)],
        2 * LANES * width * 1024,
    )[0]
    lag_sums = jnp.sum(third[:, own_rows:], axis=0)
    tap_part, cot_part = lag_sums[:own_groups], lag_sums[own_groups:]
    lam_own = lax.dynamic_slice_in_dim(lam, me * own_groups, own_groups, 0)
    local_part = jnp.sum(lam_own * cot_part[:, None, :], axis=2)
    first_part = jnp.sum(state_sums.reshape(own_rows, per, size), axis=2)
    message = jnp.concatenate(
        [tap_part.reshape(-1), local_part.reshape(-1), first_part.reshape(-1)]
    )
    pad = -message.size % LANES
    message = jnp.concatenate([message, jnp.zeros((pad,), F32)]).reshape(-1, LANES)
    got = exchange(
        jnp.broadcast_to(message[None], (reps * count,) + message.shape), ("rep", "ctx")
    )
    got = jnp.sum(got.reshape(reps, count, -1), axis=0)
    n_tap, n_loc = own_groups * LANES, own_groups * modes
    grad_taps = got[:, :n_tap].reshape(groups, LANES)
    local_all = got[:, n_tap : n_tap + n_loc].reshape(groups, modes)
    first_all = got[:, n_tap + n_loc : n_tap + n_loc + own_rows * per].reshape(tiles, modes, per)
    first_all = jnp.swapaxes(first_all, 1, 2).reshape(groups, modes)

    grad_gate_mr = call(
        bind(mixer_kernel, size), width, step, [None, None, group_rows, None], [(None, BF16)],
        [mixer_in, before, taps_back, cot], 2 * LANES * width * 1024,
    )[0]
    scale = 1.0 / math.sqrt(reps * count * LANES)
    return (
        grad_inputs[None],
        grad_gate_li[None],
        grad_gate_mr[None],
        norm * (first_all + local_all) * scale,
        grad_taps * scale,
    )


def solution(mesh):
    big = P("rep", "ctx", None)
    return jax.shard_map(
        on_device,
        mesh=mesh,
        in_specs=(big, big, big, big, P(), P(), P()),
        out_specs=(big, big, big, P(), P()),
        check_vma=False,
    )
```

```python
import functools
import math

import jax
import jax.numpy as jnp
from jax import lax
from jax.experimental import pallas as pl
from jax.experimental.pallas import tpu as pltpu
from jax.sharding import PartitionSpec as P

F32 = jnp.float32
BF16 = jnp.bfloat16
LANES = 128
NN = (((1,), (0,)), ((), ()))
NT = (((1,), (1,)), ((), ()))
TN = (((0,), (0,)), ((), ()))
VMEM_LIMIT = 60 * 1024 * 1024


def dot(left, right, dims=NN):
    return lax.dot_general(left, right, dims, preferred_element_type=F32)


def split(x):
    high = x.astype(BF16)
    return high, (x - high.astype(F32)).astype(BF16)


def iota(shape, dim):
    return lax.broadcasted_iota(jnp.int32, shape, dim)


def roll_left(x, amount):
    return pltpu.roll(x, x.shape[1] - amount, 1)


def pick_groups(stacked, rows, size):
    lane_group = iota((rows, LANES), 1) // size
    out = stacked[:rows]
    for g in range(1, LANES // size):
        out = jnp.where(lane_group == g, stacked[g * rows : (g + 1) * rows], out)
    return out


def spread_groups(x, size):
    lane_group = iota(x.shape, 1) // size
    zero = jnp.zeros_like(x)
    return jnp.concatenate(
        [jnp.where(lane_group == g, x, zero) for g in range(LANES // size)], axis=0
    )


def circulant(row):
    return split(pltpu.roll(jnp.broadcast_to(row, (LANES, LANES)), 0, 1, stride=1, stride_axis=0))


def masked(row, keeps):
    parts = circulant(row)
    zero = jnp.zeros_like(parts[0])
    return jnp.concatenate([jnp.where(keep, part, zero) for part in parts for keep in keeps], axis=1)


def toeplitz(rows_ref, i, per, keeps):
    return jnp.concatenate(
        [masked(rows_ref[i * per + g : i * per + g + 1, :], keeps) for g in range(per)], axis=0
    )


def lag_rows(z):
    sums = [None] * 4
    for k in range(LANES // 8):
        part = z[8 * k : 8 * k + 8]
        part = roll_left(part, 8 * k) if k else part
        sums[k % 4] = part if sums[k % 4] is None else sums[k % 4] + part
    return (sums[0] + sums[1]) + (sums[2] + sums[3])


def lag_sums(rows):
    rows = jnp.concatenate(rows, axis=0)
    sub = iota(rows.shape, 0)
    for bit in (4, 2, 1):
        rows = jnp.where((sub & bit) != 0, roll_left(rows, bit), rows)
    return jnp.sum(rows.reshape(-1, 8, LANES), axis=1)


def carried_part(table, entering, size):
    high, low = (spread_groups(part, size) for part in split(entering))
    return dot(
        jnp.concatenate([table, table], axis=1), jnp.concatenate([high, high, low, low], axis=0)
    )


def states_of(ref, i, modes):
    return jnp.concatenate(
        [ref[i * 2 * modes + k : i * 2 * modes + k + 4, :] for k in range(0, 2 * modes, 8)], axis=0
    )


def mode_sums(table, x, size, modes):
    high, low = split(table)
    if x.dtype == BF16:
        prod = dot(jnp.concatenate([high, low], axis=0), x)
    else:
        left = jnp.concatenate(
            [jnp.concatenate([high, high], axis=1), jnp.concatenate([low, low], axis=1)], axis=0
        )
        prod = dot(left, jnp.concatenate(split(x), axis=0))
    half = prod.shape[0] // 2
    return pick_groups(prod[:half] + prod[half:], modes, size)


def tiles_of(ref):
    return [slice(i * LANES, (i + 1) * LANES) for i in range(ref.shape[1] // LANES)]


def states_kernel(size, modes, x_ref, table_ref, out_ref):
    rows = LANES // size * modes
    out = [
        mode_sums(table_ref[i * rows : (i + 1) * rows, :], x_ref[:, lanes], size, modes)
        for i, lanes in enumerate(tiles_of(x_ref))
    ]
    out_ref[...] = jnp.concatenate(out, axis=0)


def mixer_back_kernel(
    size, modes, own_ref, next_ref, gate_ref, x_ref, taps_ref, table_ref, gm_ref, out_ref, lag_ref
):
    per = LANES // size
    rows = per * modes
    row, col = iota((LANES, LANES), 0), iota((LANES, LANES), 1)
    tiles = tiles_of(x_ref)
    cots, out, lag_parts = [], [], []
    for i, lanes in enumerate(tiles):
        own, after = own_ref[:, lanes], next_ref[:, lanes]
        left = toeplitz(taps_ref, i, per, [col >= row, col < row])
        prod = dot(left, jnp.concatenate([own, after, own, after], axis=0))
        grad_mixer = pick_groups(prod, LANES, size)
        gm_ref[:, lanes] = grad_mixer
        cots.append(grad_mixer * gate_ref[:, lanes].astype(F32))
    for i, lanes in enumerate(tiles):
        out.append(mode_sums(table_ref[i * rows : (i + 1) * rows, :], cots[i], size, modes))
    for i, lanes in enumerate(tiles):
        pairs = dot(spread_groups(x_ref[:, lanes], size), cots[i].astype(BF16), NT)
        for g in range(per):
            lag_parts.append(lag_rows(jnp.where(col >= row, pairs[g * LANES : (g + 1) * LANES], 0.0)))
    out_ref[...] = jnp.concatenate(out, axis=0)
    lag_ref[...] = lag_sums(lag_parts)


def values_kernel(
    size, modes, x_ref, gate_ref, gm_ref, own_ref, next_ref, filt_ref, table_ref, enter_ref,
    mix_ref, ggl_ref, lag_ref,
):
    per = LANES // size
    row, col = iota((LANES, LANES), 0), iota((LANES, LANES), 1)
    tiles = tiles_of(x_ref)
    values, mixes, lag_parts = [], [], []
    for i, lanes in enumerate(tiles):
        values.append(
            carried_part(
                table_ref[i * LANES : (i + 1) * LANES, :], states_of(enter_ref, i, modes), size
            )
        )
    for i, lanes in enumerate(tiles):
        x = x_ref[:, lanes]
        prod = dot(toeplitz(filt_ref, i, per, [col <= row]), jnp.concatenate([x, x], axis=0))
        full = pick_groups(prod, LANES, size) + values[i]
        ggl_ref[:, lanes] = (gm_ref[:, lanes] * full).astype(BF16)
        mixes.append((gate_ref[:, lanes].astype(F32) * full).astype(BF16))
    for i, lanes in enumerate(tiles):
        mix_ref[:, lanes] = mixes[i]
        both = jnp.concatenate([own_ref[:, lanes], next_ref[:, lanes]], axis=0)
        pairs = dot(spread_groups(mixes[i], size), both, NT)
        for g in range(per):
            z = pairs[g * LANES : (g + 1) * LANES]
            lag_parts.append(lag_rows(jnp.where(col >= row, z[:, :LANES], z[:, LANES:])))
    lag_ref[...] = lag_sums(lag_parts)


def input_grad_kernel(size, modes, gm_ref, gate_ref, filt_ref, table_ref, enter_ref, out_ref):
    per = LANES // size
    row, col = iota((LANES, LANES), 0), iota((LANES, LANES), 1)
    for i, lanes in enumerate(tiles_of(gm_ref)):
        left = toeplitz(filt_ref, i, per, [col >= row])
        high, low = split(gm_ref[:, lanes] * gate_ref[:, lanes].astype(F32))
        prod = dot(
            jnp.concatenate([left, left[:, :LANES]], axis=1), jnp.concatenate([high, high, low], axis=0)
        )
        out_ref[:, lanes] = (
            pick_groups(prod, LANES, size)
            + carried_part(
                table_ref[i * LANES : (i + 1) * LANES, :], states_of(enter_ref, i, modes), size
            )
        ).astype(BF16)


def mixer_kernel(size, own_ref, before_ref, taps_ref, cot_ref, out_ref):
    per = LANES // size
    row, col = iota((LANES, LANES), 0), iota((LANES, LANES), 1)
    for i, lanes in enumerate(tiles_of(own_ref)):
        own, before = own_ref[:, lanes], before_ref[:, lanes]
        left = toeplitz(taps_ref, i, per, [col <= row, col > row])
        prod = dot(left, jnp.concatenate([own, before, own, before], axis=0))
        mixed = pick_groups(prod, LANES, size)
        out_ref[:, lanes] = (cot_ref[:, lanes].astype(F32) * mixed).astype(BF16)


def scan_kernel(x_ref, decay_ref, beside_ref, out_ref):
    decay = decay_ref[...]
    rows = decay.shape[0]
    state = jnp.zeros_like(decay)
    for d in range(x_ref.shape[0]):
        out_ref[d, :rows, :] = state
        out_ref[d, rows:, :] = beside_ref[d]
        state = decay * state + x_ref[d]


def back_scan_kernel(x_ref, decay_ref, front_ref, tap_ref, cot_ref, out_ref, sum_ref):
    decay = decay_ref[...]
    rows = decay.shape[0]
    per = tap_ref.shape[0] // x_ref.shape[0]
    state = jnp.zeros_like(decay)
    total = jnp.zeros_like(decay)
    rest = jnp.zeros((rows - 2 * per, LANES), F32)
    for d in reversed(range(x_ref.shape[0])):
        x = x_ref[d, rows:, :]
        out_ref[d, :rows, :] = state
        out_ref[d, rows:, :] = jnp.concatenate(
            [tap_ref[d * per : (d + 1) * per, :], cot_ref[d * per : (d + 1) * per, :], rest], axis=0
        )
        state = decay * state + x
        total = total + x * front_ref[d, :rows, :]
    sum_ref[...] = total


def collect_kernel(size, x_ref, sum_ref, lam_ref, out_ref):
    rows, modes = sum_ref.shape[0], lam_ref.shape[0]
    lags = jnp.sum(x_ref[:, rows:, :], axis=0)
    exact = functools.partial(
        lax.dot_general, precision=lax.Precision.HIGHEST, preferred_element_type=F32
    )
    lam = jnp.concatenate([lam_ref[...], jnp.zeros((LANES - modes, LANES), F32)], axis=0)
    second = exact(jnp.broadcast_to(lags[1:2], (8, LANES)), lam, NT)[:1]
    lane, place = iota((LANES, LANES), 0), iota((LANES, LANES), 1)
    per = LANES // size
    for q in range(rows):
        pick = (place == modes + q * per + lane // size).astype(F32)
        second = second + exact(jnp.broadcast_to(sum_ref[q : q + 1, :], (8, LANES)), pick, NN)[:1]
    message = jnp.concatenate([lags[:1], second], axis=0)
    out_ref[...] = jnp.broadcast_to(message[None], out_ref.shape)


def call(body, width, step, chunk, specs, outs, args, micros):
    kinds = list(specs) + [rows for rows, kind in outs]
    chunks = step // chunk

    def kernel(*refs):
        def part(c, carry):
            views = []
            for ref, rows in zip(refs, kinds):
                if rows is None:
                    views.append(ref.at[:, pl.ds(pl.multiple_of(c * chunk, chunk), chunk)])
                else:
                    views.append(ref.at[pl.ds(pl.multiple_of(c * rows, rows), rows), :])
            body(*views)
            return carry

        lax.fori_loop(0, chunks, part, 0)

    def block(rows):
        if rows is None:
            return pl.BlockSpec((LANES, step), lambda i: (0, i))
        return pl.BlockSpec((rows * chunks, LANES), lambda i: (i, 0))

    def shape(rows, kind):
        if rows is None:
            return jax.ShapeDtypeStruct((LANES, width), kind)
        return jax.ShapeDtypeStruct((rows * (width // chunk), LANES), kind)

    nbytes = sum(a.size * a.dtype.itemsize for a in args)
    return pl.pallas_call(
        kernel,
        grid=(width // step,),
        in_specs=[block(rows) for rows in specs],
        out_specs=[block(rows) for rows, kind in outs],
        out_shape=[shape(rows, kind) for rows, kind in outs],
        compiler_params=pltpu.CompilerParams(vmem_limit_bytes=VMEM_LIMIT),
        cost_estimate=pl.CostEstimate(flops=micros * 1_000_000_000, bytes_accessed=nbytes, transcendentals=0),
    )(*args)


def whole(body, outs, args):
    return pl.pallas_call(
        body,
        out_shape=[jax.ShapeDtypeStruct(s, F32) for s in outs],
        compiler_params=pltpu.CompilerParams(vmem_limit_bytes=VMEM_LIMIT),
    )(*args)


def shifted(x, by):
    count = lax.axis_size("ctx")
    return lax.ppermute(x, "ctx", [(i, i + by) for i in range(count) if 0 <= i + by < count])


def exchange(x, axes="ctx"):
    return lax.all_to_all(x, axes, split_axis=0, concat_axis=0, tiled=True)


def carry_table(x):
    return jnp.concatenate(split(x), axis=2).reshape(-1, 2 * x.shape[2])


def on_device(inputs, gate_li, gate_mr, cotangent, residues, rates, taps):
    seq, gate, cot = inputs[0], gate_li[0], cotangent[0]
    width = seq.shape[1]
    groups, modes = rates.shape
    size = width // groups
    per = LANES // size
    tiles = width // LANES
    reps, count = lax.axis_size("rep"), lax.axis_size("ctx")
    me = lax.axis_index("ctx")
    own_rows = tiles * modes // count
    step, chunk = min(2048, width), min(1024, width)
    state_rows = chunk // LANES * modes
    table_rows = per * state_rows
    group_rows = chunk // size
    carry_rows = chunk

    scaled = (cot.astype(F32) * gate_mr[0].astype(F32)).astype(BF16)
    after = shifted(scaled, -1)

    lags = jnp.arange(LANES).astype(F32)
    norm = jnp.sqrt(-jnp.expm1(-2.0 * rates))
    weight = residues * norm
    rate3, weight3 = rates[:, :, None], weight[:, :, None]
    lam = jnp.exp(-rate3 * lags)
    filt = jnp.sum(weight3 * lam, axis=1)
    filt_back = jnp.roll(jnp.flip(filt, 1), 1, axis=1)
    taps_back = jnp.roll(jnp.flip(taps, 1), 1, axis=1)
    to_end = jnp.exp(-rate3 * (LANES - 1.0 - lags))
    from_start = jnp.exp(-rate3 * (lags + 1.0))
    flat = (groups * modes, LANES)
    end_table = to_end.reshape(flat)
    start_table = from_start.reshape(flat)
    rate_row = rates.reshape(tiles, 1, per * modes)
    weight_row = weight.reshape(tiles, 1, per * modes)
    front_table = carry_table(weight_row * jnp.exp(-rate_row * (lags[:, None] + 1.0)))
    back_table = carry_table(weight_row * jnp.exp(-rate_row * (LANES - 1.0 - lags[:, None])))
    decay = jnp.exp(-rates * LANES).reshape(tiles, per, modes)
    decay = jnp.repeat(jnp.swapaxes(decay, 1, 2).reshape(tiles * modes, per), size, axis=1)
    decay = lax.dynamic_slice_in_dim(decay, me * own_rows, own_rows, 0)

    bind = functools.partial
    states = call(
        bind(states_kernel, size, modes), width, step, chunk, [None, table_rows], [(state_rows, F32)],
        [seq, end_table], 3,
    )[0]
    ends = exchange(states.reshape(count, own_rows, LANES))

    grad_mixer, back_states, lag_cot = call(
        bind(mixer_back_kernel, size, modes), width, step, chunk,
        [None, None, None, None, group_rows, table_rows],
        [(None, F32), (state_rows, F32), (group_rows, F32)],
        [scaled, after, gate, seq, taps, start_table], 11,
    )
    first = whole(
        scan_kernel, [(count, 2 * own_rows, LANES)],
        [ends, decay, back_states.reshape(count, own_rows, LANES)],
    )[0]
    second = exchange(first)
    mixer_in, grad_gate_li, lag_taps = call(
        bind(values_kernel, size, modes), width, step, chunk,
        [None, None, None, None, None, group_rows, carry_rows, 2 * state_rows],
        [(None, BF16), (None, BF16), (group_rows, F32)],
        [seq, gate, grad_mixer, scaled, after, filt_back, front_table, second.reshape(-1, LANES)], 10,
    )
    before = shifted(mixer_in, 1)
    message, state_sums = whole(
        back_scan_kernel, [first.shape, decay.shape], [second, decay, first, lag_taps, lag_cot]
    )
    third = exchange(message)
    own_groups = groups // count
    lam_own = lax.dynamic_slice_in_dim(lam, me * own_groups, own_groups, 0).reshape(modes, LANES)
    spread = whole(
        bind(collect_kernel, size), [(reps * count, 2, LANES)], [third, state_sums, lam_own]
    )[0]
    got = exchange(spread, ("rep", "ctx"))
    grad_inputs = call(
        bind(input_grad_kernel, size, modes), width, step, chunk,
        [None, None, group_rows, carry_rows, 2 * state_rows], [(None, BF16)],
        [grad_mixer, gate, filt, back_table, third.reshape(-1, LANES)], 6,
    )[0]
    grad_gate_mr = call(
        bind(mixer_kernel, size), width, step, chunk, [None, None, group_rows, None], [(None, BF16)],
        [mixer_in, before, taps_back, cot], 7,
    )[0]
    got = jnp.sum(got.reshape(reps, count, 2, LANES), axis=0)
    local_all = got[:, 1, :modes]
    first_all = got[:, 1, modes : modes + own_rows * per].reshape(tiles, modes, per)
    first_all = jnp.swapaxes(first_all, 1, 2).reshape(groups, modes)
    scale = 1.0 / math.sqrt(reps * count * LANES)
    return (
        grad_inputs[None],
        grad_gate_li[None],
        grad_gate_mr[None],
        norm * (first_all + local_all) * scale,
        got[:, 0] * scale,
    )


def solution(mesh):
    big = P("rep", "ctx", None)
    return jax.shard_map(
        on_device,
        mesh=mesh,
        in_specs=(big, big, big, big, P(), P(), P()),
        out_specs=(big, big, big, P(), P()),
        check_vma=False,
    )
```

```python
import functools
import math

import jax
import jax.numpy as jnp
from jax import lax
from jax.experimental import pallas as pl
from jax.experimental.pallas import tpu as pltpu
from jax.sharding import PartitionSpec as P

F32 = jnp.float32
BF16 = jnp.bfloat16
LANES = 128
NN = (((1,), (0,)), ((), ()))
NT = (((1,), (1,)), ((), ()))
TN = (((0,), (0,)), ((), ()))


def dot(left, right, dims=NN):
    return lax.dot_general(left, right, dims, preferred_element_type=F32)


def split(x):
    high = x.astype(BF16)
    return high, (x - high.astype(F32)).astype(BF16)


def iota(shape, dim):
    return lax.broadcasted_iota(jnp.int32, shape, dim)


def roll_left(x, amount):
    return pltpu.roll(x, x.shape[1] - amount, 1)


def pick_groups(stacked, rows, size):
    lane_group = iota((rows, LANES), 1) // size
    out = stacked[:rows]
    for g in range(1, LANES // size):
        out = jnp.where(lane_group == g, stacked[g * rows : (g + 1) * rows], out)
    return out


def spread_groups(x, size):
    lane_group = iota(x.shape, 1) // size
    zero = jnp.zeros_like(x)
    return jnp.concatenate(
        [jnp.where(lane_group == g, x, zero) for g in range(LANES // size)], axis=0
    )


def circulant(row):
    return split(pltpu.roll(jnp.broadcast_to(row, (LANES, LANES)), 0, 1, stride=1, stride_axis=0))


def masked(row, keeps):
    parts = circulant(row)
    zero = jnp.zeros_like(parts[0])
    return jnp.concatenate([jnp.where(keep, part, zero) for part in parts for keep in keeps], axis=1)


def toeplitz(rows_ref, i, per, keeps):
    return jnp.concatenate(
        [masked(rows_ref[i * per + g : i * per + g + 1, :], keeps) for g in range(per)], axis=0
    )


def lag_rows(z):
    sums = [None] * 4
    for k in range(LANES // 8):
        part = z[8 * k : 8 * k + 8]
        part = roll_left(part, 8 * k) if k else part
        sums[k % 4] = part if sums[k % 4] is None else sums[k % 4] + part
    return (sums[0] + sums[1]) + (sums[2] + sums[3])


def lag_sums(rows):
    rows = jnp.concatenate(rows, axis=0)
    sub = iota(rows.shape, 0)
    for bit in (4, 2, 1):
        rows = jnp.where((sub & bit) != 0, roll_left(rows, bit), rows)
    return jnp.sum(rows.reshape(-1, 8, LANES), axis=1)


def carried_part(table, ref, i, modes, size):
    x = ref[i * 2 * modes : (i + 1) * 2 * modes, :].astype(F32)
    x = jnp.concatenate([x[k : k + 4] for k in range(0, 2 * modes, 8)], axis=0)
    x = spread_groups(x, size).astype(BF16)
    return dot(table, jnp.concatenate([x, x], axis=0))


def mode_sums(table, x, size, modes):
    high, low = split(table)
    if x.dtype == BF16:
        prod = dot(jnp.concatenate([high, low], axis=0), x)
    else:
        left = jnp.concatenate(
            [jnp.concatenate([high, high], axis=1), jnp.concatenate([low, low], axis=1)], axis=0
        )
        prod = dot(left, jnp.concatenate(split(x), axis=0))
    half = prod.shape[0] // 2
    return pick_groups(prod[:half] + prod[half:], modes, size)


def tiles_of(ref):
    return [slice(i * LANES, (i + 1) * LANES) for i in range(ref.shape[1] // LANES)]


def states_kernel(size, modes, x_ref, table_ref, out_ref):
    rows = LANES // size * modes
    out = [
        mode_sums(table_ref[i * rows : (i + 1) * rows, :], x_ref[:, lanes], size, modes)
        for i, lanes in enumerate(tiles_of(x_ref))
    ]
    out_ref[...] = jnp.concatenate(out, axis=0)


def mixer_back_kernel(
    size, modes, own_ref, next_ref, gate_ref, x_ref, taps_ref, table_ref, gm_ref, out_ref, lag_ref
):
    per = LANES // size
    rows = per * modes
    row, col = iota((LANES, LANES), 0), iota((LANES, LANES), 1)
    tiles = tiles_of(x_ref)
    cots, out, lag_parts = [], [], []
    for i, lanes in enumerate(tiles):
        own, after = own_ref[:, lanes], next_ref[:, lanes]
        left = toeplitz(taps_ref, i, per, [col >= row, col < row])
        prod = dot(left, jnp.concatenate([own, after, own, after], axis=0))
        grad_mixer = pick_groups(prod, LANES, size)
        gm_ref[:, lanes] = grad_mixer
        cots.append(grad_mixer * gate_ref[:, lanes].astype(F32))
    for i, lanes in enumerate(tiles):
        out.append(mode_sums(table_ref[i * rows : (i + 1) * rows, :], cots[i], size, modes))
    for i, lanes in enumerate(tiles):
        pairs = dot(spread_groups(x_ref[:, lanes], size), cots[i].astype(BF16), NT)
        for g in range(per):
            lag_parts.append(lag_rows(jnp.where(col >= row, pairs[g * LANES : (g + 1) * LANES], 0.0)))
    out_ref[...] = jnp.concatenate(out, axis=0)
    lag_ref[...] = lag_sums(lag_parts)


def local_kernel(size, x_ref, filt_ref, rate_ref, weight_ref, out_ref, front_ref, back_ref):
    per = LANES // size
    row, col = iota((LANES, LANES), 0), iota((LANES, LANES), 1)
    up = row.astype(F32)
    for i, lanes in enumerate(tiles_of(x_ref)):
        x = x_ref[:, lanes]
        prod = dot(toeplitz(filt_ref, i, per, [col <= row]), jnp.concatenate([x, x], axis=0))
        out_ref[:, lanes] = pick_groups(prod, LANES, size)
    for i in range(x_ref.shape[1] // LANES):
        rate, weight = rate_ref[i : i + 1, :], weight_ref[i : i + 1, :]
        for ref, steps in ((front_ref, up + 1.0), (back_ref, LANES - 1.0 - up)):
            high, low = split(weight * jnp.exp(-rate * steps))
            ref[i * LANES : (i + 1) * LANES, :] = jnp.where(col < LANES // 2, high, low)


def values_kernel(
    size, modes, local_ref, gate_ref, gm_ref, own_ref, next_ref, table_ref, enter_ref,
    mix_ref, ggl_ref, lag_ref,
):
    per = LANES // size
    row, col = iota((LANES, LANES), 0), iota((LANES, LANES), 1)
    tiles = tiles_of(local_ref)
    mixes, lag_parts = [], []
    for i, lanes in enumerate(tiles):
        table = table_ref[i * LANES : (i + 1) * LANES, :]
        full = local_ref[:, lanes] + carried_part(table, enter_ref, i, modes, size)
        ggl_ref[:, lanes] = (gm_ref[:, lanes] * full).astype(BF16)
        mixes.append((gate_ref[:, lanes].astype(F32) * full).astype(BF16))
    for i, lanes in enumerate(tiles):
        mix_ref[:, lanes] = mixes[i]
        both = jnp.concatenate([own_ref[:, lanes], next_ref[:, lanes]], axis=0)
        pairs = dot(spread_groups(mixes[i], size), both, NT)
        for g in range(per):
            z = pairs[g * LANES : (g + 1) * LANES]
            lag_parts.append(lag_rows(jnp.where(col >= row, z[:, :LANES], z[:, LANES:])))
    lag_ref[...] = lag_sums(lag_parts)


def input_grad_kernel(size, modes, gm_ref, gate_ref, filt_ref, table_ref, enter_ref, out_ref):
    per = LANES // size
    row, col = iota((LANES, LANES), 0), iota((LANES, LANES), 1)
    for i, lanes in enumerate(tiles_of(gm_ref)):
        left = toeplitz(filt_ref, i, per, [col >= row])
        high, low = split(gm_ref[:, lanes] * gate_ref[:, lanes].astype(F32))
        prod = dot(
            jnp.concatenate([left, left[:, :LANES]], axis=1), jnp.concatenate([high, high, low], axis=0)
        )
        table = table_ref[i * LANES : (i + 1) * LANES, :]
        carried = carried_part(table, enter_ref, i, modes, size)
        out_ref[:, lanes] = (pick_groups(prod, LANES, size) + carried).astype(BF16)


def mixer_kernel(size, own_ref, before_ref, taps_ref, cot_ref, out_ref):
    per = LANES // size
    row, col = iota((LANES, LANES), 0), iota((LANES, LANES), 1)
    for i, lanes in enumerate(tiles_of(own_ref)):
        own, before = own_ref[:, lanes], before_ref[:, lanes]
        left = toeplitz(taps_ref, i, per, [col <= row, col > row])
        prod = dot(left, jnp.concatenate([own, before, own, before], axis=0))
        mixed = pick_groups(prod, LANES, size)
        out_ref[:, lanes] = (cot_ref[:, lanes].astype(F32) * mixed).astype(BF16)


def exact_dot(left, right, dims=NN):
    return lax.dot_general(
        left, right, dims, precision=lax.Precision.HIGHEST, preferred_element_type=F32
    )


def prepare_kernel(
    size, own_rows, me_ref, rates_ref, weight_ref, taps_ref, filt_ref, filt_back_ref, taps_back_ref,
    decay_ref, lam_ref,
):
    me = me_ref[0, 0]
    rates, taps = rates_ref[...], taps_ref[...]
    groups, modes = rates.shape
    lag = iota((groups, LANES), 1).astype(F32)
    filt = jnp.zeros((groups, LANES), F32)
    for m in range(modes):
        filt = filt + weight_ref[:, m : m + 1] * jnp.exp(-rates[:, m : m + 1] * lag)
    row, col = iota((LANES, LANES), 0), iota((LANES, LANES), 1)
    mirror = ((row + col) % LANES == 0).astype(F32)
    filt_ref[...] = filt
    filt_back_ref[...] = exact_dot(filt, mirror)
    taps_back_ref[...] = exact_dot(taps, mirror)
    per, parts = LANES // size, modes // own_rows
    pick = iota((8, modes), 1) == me % parts * own_rows + iota((8, modes), 0)
    chosen = exact_dot(pick.astype(F32), rates, NT)
    spread = iota((groups, LANES), 0) == me // parts * per + iota((groups, LANES), 1) // size
    decay_ref[...] = jnp.exp(-exact_dot(chosen, spread.astype(F32))[:own_rows] * LANES)
    own = (iota((groups, LANES), 0) == me).astype(F32)
    lam_ref[...] = jnp.exp(-exact_dot(rates, own, TN) * iota((modes, LANES), 1).astype(F32))


def scan_kernel(x_ref, decay_ref, beside_ref, out_ref, state_ref):
    decay = decay_ref[...]
    state = jnp.zeros_like(decay)
    for d in range(x_ref.shape[0]):
        state_ref[d] = state
        out_ref[d] = jnp.concatenate([state, beside_ref[d]], axis=0).astype(BF16)
        state = decay * state + x_ref[d]


def back_scan_kernel(x_ref, decay_ref, front_ref, tap_ref, cot_ref, out_ref, sum_ref):
    decay = decay_ref[...]
    rows = decay.shape[0]
    per = tap_ref.shape[0] // x_ref.shape[0]
    state = jnp.zeros_like(decay)
    total = jnp.zeros_like(decay)
    for d in reversed(range(x_ref.shape[0])):
        x = x_ref[d].astype(F32)[rows:]
        lags = jnp.concatenate(
            [tap_ref[d * per : (d + 1) * per, :], cot_ref[d * per : (d + 1) * per, :]], axis=0
        )
        low = lags - lags.astype(BF16).astype(F32)
        out_ref[d] = jnp.concatenate([state, lags, low], axis=0).astype(BF16)
        state = decay * state + x
        total = total + x * front_ref[d]
    sum_ref[...] = total


def collect_kernel(size, x_ref, sum_ref, lam_ref, out_ref):
    rows, modes = sum_ref.shape[0], lam_ref.shape[0]
    lags = jnp.sum(x_ref[...].astype(F32), axis=0)[rows:]
    lags = lags[:2] + lags[2:]
    lam = jnp.concatenate([lam_ref[...], jnp.zeros((LANES - modes, LANES), F32)], axis=0)
    second = exact_dot(jnp.broadcast_to(lags[1:2], (8, LANES)), lam, NT)[:1]
    lane, place = iota((LANES, LANES), 0), iota((LANES, LANES), 1)
    for q in range(rows):
        pick = (place == modes + lane // size * rows + q).astype(F32)
        second = second + exact_dot(jnp.broadcast_to(sum_ref[q : q + 1, :], (8, LANES)), pick, NN)[:1]
    message = jnp.concatenate([lags[:1], second], axis=0)
    out_ref[...] = jnp.broadcast_to(message[None], out_ref.shape)


def finish_kernel(scale, per, rows, x_ref, norm_ref, res_ref, tap_ref):
    count, modes = norm_ref.shape
    x = x_ref[0:count]
    for k in range(count, x_ref.shape[0], count):
        x = x + x_ref[k : k + count]
    tap_ref[...] = x[:, 0, :] * scale
    rest = x[:, 1, :]
    total = rest
    h, j = iota(rest.shape, 0) % per, iota(rest.shape, 1) // rows
    for delta in range(1 - per, per):
        moved = rest if delta == 0 else pltpu.roll(rest, delta % count, 0)
        moved = pltpu.roll(moved, (-modes - rows * delta) % LANES, 1)
        total = total + jnp.where(h - j == delta, moved, 0.0)
    res_ref[...] = total[:, :modes] * norm_ref[...] * scale


def call(body, width, step, chunk, specs, outs, args, micros, room=60):
    kinds = list(specs) + [rows for rows, kind in outs]
    chunks = step // chunk

    def kernel(*refs):
        def part(c, carry):
            views = []
            for ref, rows in zip(refs, kinds):
                if rows is None:
                    views.append(ref.at[:, pl.ds(pl.multiple_of(c * chunk, chunk), chunk)])
                else:
                    views.append(ref.at[pl.ds(pl.multiple_of(c * rows, rows), rows), :])
            body(*views)
            return carry

        lax.fori_loop(0, chunks, part, 0)

    def block(rows):
        if rows is None:
            return pl.BlockSpec((LANES, step), lambda i: (0, i))
        return pl.BlockSpec((rows * chunks, LANES), lambda i: (i, 0))

    def shape(rows, kind):
        if rows is None:
            return jax.ShapeDtypeStruct((LANES, width), kind)
        return jax.ShapeDtypeStruct((rows * (width // chunk), LANES), kind)

    nbytes = sum(a.size * a.dtype.itemsize for a in args)
    return pl.pallas_call(
        kernel,
        grid=(width // step,),
        in_specs=[block(rows) for rows in specs],
        out_specs=[block(rows) for rows, kind in outs],
        out_shape=[shape(rows, kind) for rows, kind in outs],
        compiler_params=pltpu.CompilerParams(vmem_limit_bytes=room * 1024 * 1024),
        cost_estimate=pl.CostEstimate(flops=micros * 1_000_000_000, bytes_accessed=nbytes, transcendentals=0),
    )(*args)


def whole(body, outs, args):
    return pl.pallas_call(
        body,
        out_shape=[jax.ShapeDtypeStruct(shape, kind) for shape, kind in outs],
        compiler_params=pltpu.CompilerParams(vmem_limit_bytes=8 * 1024 * 1024),
        cost_estimate=pl.CostEstimate(flops=2_000_000_000, bytes_accessed=1 << 20, transcendentals=0),
    )(*args)


def shifted(x, by):
    count = lax.axis_size("ctx")
    return lax.ppermute(x, "ctx", [(i, i + by) for i in range(count) if 0 <= i + by < count])


def exchange(x, axes="ctx"):
    return lax.all_to_all(x, axes, split_axis=0, concat_axis=0, tiled=True)


def on_device(inputs, gate_li, gate_mr, cotangent, residues, rates, taps):
    seq, gate, cot = inputs[0], gate_li[0], cotangent[0]
    width = seq.shape[1]
    groups, modes = rates.shape
    size = width // groups
    per = LANES // size
    tiles = width // LANES
    reps, count = lax.axis_size("rep"), lax.axis_size("ctx")
    me = lax.axis_index("ctx")
    own_rows = tiles * modes // count
    step, chunk = min(2048, width), min(1024, width)
    state_rows = chunk // LANES * modes
    table_rows = per * state_rows
    group_rows = chunk // size
    carry_rows, tile_rows = chunk, chunk // LANES

    scaled = (cot.astype(F32) * gate_mr[0].astype(F32)).astype(BF16)
    after = shifted(scaled, -1)

    lags = jnp.arange(LANES).astype(F32)
    norm = jnp.sqrt(-jnp.expm1(-2.0 * rates))
    weight = residues * norm
    rate3, weight3 = rates[:, :, None], weight[:, :, None]
    to_end = jnp.exp(-rate3 * (LANES - 1.0 - lags))
    from_start = jnp.exp(-rate3 * (lags + 1.0))
    flat = (groups * modes, LANES)
    end_table = to_end.reshape(flat)
    start_table = from_start.reshape(flat)
    rate_row = rates.reshape(tiles, per * modes)
    rate_row = jnp.concatenate([rate_row, rate_row], axis=1)
    weight_row = weight.reshape(tiles, per * modes)
    weight_row = jnp.concatenate([weight_row, weight_row], axis=1)
    filt, filt_back, taps_back, decay, lam_own = pl.pallas_call(
        functools.partial(prepare_kernel, size, own_rows),
        in_specs=[pl.BlockSpec(memory_space=pltpu.SMEM)] + [pl.BlockSpec(memory_space=pltpu.VMEM)] * 3,
        out_shape=[
            jax.ShapeDtypeStruct(shape, F32)
            for shape in (taps.shape, taps.shape, taps.shape, (own_rows, LANES), (modes, LANES))
        ],
        compiler_params=pltpu.CompilerParams(vmem_limit_bytes=8 * 1024 * 1024),
        cost_estimate=pl.CostEstimate(flops=3_000_000_000, bytes_accessed=1 << 20, transcendentals=0),
    )(me.astype(jnp.int32).reshape(1, 1), rates, weight, taps)

    bind = functools.partial
    states = call(
        bind(states_kernel, size, modes), width, step, chunk, [None, table_rows], [(state_rows, F32)],
        [seq, end_table], 3,
    )[0]
    ends = exchange(states.reshape(count, own_rows, LANES))

    after, filt, filt_back, taps_back, decay, lam_own = lax.optimization_barrier(
        (after, filt, filt_back, taps_back, decay, lam_own)
    )
    grad_mixer, back_states, lag_cot = call(
        bind(mixer_back_kernel, size, modes), width, step, chunk,
        [None, None, None, None, group_rows, table_rows],
        [(None, F32), (state_rows, F32), (group_rows, F32)],
        [scaled, after, gate, seq, taps, start_table], 11,
    )
    first, entering = whole(
        scan_kernel, [((count, 2 * own_rows, LANES), BF16), (ends.shape, F32)],
        [ends, decay, back_states.reshape(count, own_rows, LANES)],
    )
    second = exchange(first)
    local, front_table, back_table = call(
        bind(local_kernel, size), width, step, chunk,
        [None, group_rows, tile_rows, tile_rows], [(None, F32), (carry_rows, BF16), (carry_rows, BF16)],
        [seq, filt_back, rate_row, weight_row], 7,
    )
    mixer_in, grad_gate_li, lag_taps = call(
        bind(values_kernel, size, modes), width, step, chunk,
        [None, None, None, None, None, carry_rows, 2 * state_rows],
        [(None, BF16), (None, BF16), (group_rows, F32)],
        [local, gate, grad_mixer, scaled, after, front_table, second.reshape(-1, LANES)], 6,
    )
    before = shifted(mixer_in, 1)
    message, state_sums = whole(
        back_scan_kernel, [(first.shape, BF16), (decay.shape, F32)],
        [second, decay, entering, lag_taps, lag_cot],
    )
    third = exchange(message)
    grad_gate_mr = call(
        bind(mixer_kernel, size), width, step, chunk, [None, None, group_rows, None], [(None, BF16)],
        [mixer_in, before, taps_back, cot], 7, 32,
    )[0]
    third, grad_gate_mr = lax.optimization_barrier((third, grad_gate_mr))
    spread = whole(
        bind(collect_kernel, size), [((reps * count, 2, LANES), F32)], [third, state_sums, lam_own]
    )[0]
    got = exchange(spread, ("rep", "ctx"))
    grad_inputs = call(
        bind(input_grad_kernel, size, modes), width, step, chunk,
        [None, None, group_rows, carry_rows, 2 * state_rows], [(None, BF16)],
        [grad_mixer, gate, filt, back_table, third.reshape(-1, LANES)], 7,
    )[0]
    grad_residues, grad_taps = whole(
        bind(finish_kernel, 1.0 / math.sqrt(reps * count * LANES), per, own_rows),
        [(rates.shape, F32), (taps.shape, F32)], [got, norm],
    )
    return grad_inputs[None], grad_gate_li[None], grad_gate_mr[None], grad_residues, grad_taps


def solution(mesh):
    big = P("rep", "ctx", None)
    return jax.shard_map(
        on_device,
        mesh=mesh,
        in_specs=(big, big, big, big, P(), P(), P()),
        out_specs=(big, big, big, P(), P()),
        check_vma=False,
    )
```

```python
import functools
import math

import jax
import jax.numpy as jnp
from jax import lax
from jax.experimental import pallas as pl
from jax.experimental.pallas import tpu as pltpu
from jax.sharding import PartitionSpec as P

F32 = jnp.float32
BF16 = jnp.bfloat16
LANES = 128
NN = (((1,), (0,)), ((), ()))
NT = (((1,), (1,)), ((), ()))
TN = (((0,), (0,)), ((), ()))


def dot(left, right, dims=NN):
    return lax.dot_general(left, right, dims, preferred_element_type=F32)


def split(x):
    high = x.astype(BF16)
    return high, (x - high.astype(F32)).astype(BF16)


def iota(shape, dim):
    return lax.broadcasted_iota(jnp.int32, shape, dim)


def roll_left(x, amount):
    return pltpu.roll(x, x.shape[1] - amount, 1)


def pick_groups(stacked, rows, size):
    lane_group = iota((rows, LANES), 1) // size
    out = stacked[:rows]
    for g in range(1, LANES // size):
        out = jnp.where(lane_group == g, stacked[g * rows : (g + 1) * rows], out)
    return out


def spread_groups(x, size):
    lane_group = iota(x.shape, 1) // size
    zero = jnp.zeros_like(x)
    return jnp.concatenate(
        [jnp.where(lane_group == g, x, zero) for g in range(LANES // size)], axis=0
    )


def circulant(row):
    return split(pltpu.roll(jnp.broadcast_to(row, (LANES, LANES)), 0, 1, stride=1, stride_axis=0))


def masked(row, keeps):
    parts = circulant(row)
    zero = jnp.zeros_like(parts[0])
    return jnp.concatenate([jnp.where(keep, part, zero) for part in parts for keep in keeps], axis=1)


def toeplitz(rows_ref, i, per, keeps):
    return jnp.concatenate(
        [masked(rows_ref[i * per + g : i * per + g + 1, :], keeps) for g in range(per)], axis=0
    )


def lag_rows(z):
    sums = [None] * 4
    for k in range(LANES // 8):
        part = z[8 * k : 8 * k + 8]
        part = roll_left(part, 8 * k) if k else part
        sums[k % 4] = part if sums[k % 4] is None else sums[k % 4] + part
    return (sums[0] + sums[1]) + (sums[2] + sums[3])


def lag_sums(rows):
    rows = jnp.concatenate(rows, axis=0)
    sub = iota(rows.shape, 0)
    for bit in (4, 2, 1):
        rows = jnp.where((sub & bit) != 0, roll_left(rows, bit), rows)
    return jnp.sum(rows.reshape(-1, 8, LANES), axis=1)


def carried_part(table, ref, i, modes, size):
    x = ref[i * 2 * modes : (i + 1) * 2 * modes, :].astype(F32)
    x = jnp.concatenate([x[k : k + 4] for k in range(0, 2 * modes, 8)], axis=0)
    x = spread_groups(x, size).astype(BF16)
    return dot(table, jnp.concatenate([x, x], axis=0))


def mode_sums(table, x, size, modes):
    high, low = split(table)
    if x.dtype == BF16:
        prod = dot(jnp.concatenate([high, low], axis=0), x)
    else:
        left = jnp.concatenate(
            [jnp.concatenate([high, high], axis=1), jnp.concatenate([low, low], axis=1)], axis=0
        )
        prod = dot(left, jnp.concatenate(split(x), axis=0))
    half = prod.shape[0] // 2
    return pick_groups(prod[:half] + prod[half:], modes, size)


def tiles_of(ref):
    return [slice(i * LANES, (i + 1) * LANES) for i in range(ref.shape[1] // LANES)]


def states_kernel(size, modes, x_ref, table_ref, out_ref):
    rows = LANES // size * modes
    out = [
        mode_sums(table_ref[i * rows : (i + 1) * rows, :], x_ref[:, lanes], size, modes)
        for i, lanes in enumerate(tiles_of(x_ref))
    ]
    out_ref[...] = jnp.concatenate(out, axis=0)


def mixer_back_kernel(size, modes, own_ref, next_ref, gate_ref, taps_ref, table_ref, gm_ref, out_ref):
    per = LANES // size
    rows = per * modes
    row, col = iota((LANES, LANES), 0), iota((LANES, LANES), 1)
    tiles = tiles_of(own_ref)
    cots, out = [], []
    for i, lanes in enumerate(tiles):
        own, after = own_ref[:, lanes], next_ref[:, lanes]
        left = toeplitz(taps_ref, i, per, [col >= row, col < row])
        prod = dot(left, jnp.concatenate([own, after, own, after], axis=0))
        grad_mixer = pick_groups(prod, LANES, size)
        gm_ref[:, lanes] = grad_mixer
        cots.append(grad_mixer * gate_ref[:, lanes].astype(F32))
    for i, lanes in enumerate(tiles):
        out.append(mode_sums(table_ref[i * rows : (i + 1) * rows, :], cots[i], size, modes))
    out_ref[...] = jnp.concatenate(out, axis=0)


def local_kernel(
    size, x_ref, gate_ref, gm_ref, filt_ref, rate_ref, weight_ref,
    out_ref, front_ref, back_ref, lag_ref,
):
    per = LANES // size
    row, col = iota((LANES, LANES), 0), iota((LANES, LANES), 1)
    up = row.astype(F32)
    tiles = tiles_of(x_ref)
    lag_parts = []
    for i, lanes in enumerate(tiles):
        x = x_ref[:, lanes]
        prod = dot(toeplitz(filt_ref, i, per, [col <= row]), jnp.concatenate([x, x], axis=0))
        out_ref[:, lanes] = pick_groups(prod, LANES, size)
    for i in range(len(tiles)):
        rate, weight = rate_ref[i : i + 1, :], weight_ref[i : i + 1, :]
        for ref, steps in ((front_ref, up + 1.0), (back_ref, LANES - 1.0 - up)):
            high, low = split(weight * jnp.exp(-rate * steps))
            ref[i * LANES : (i + 1) * LANES, :] = jnp.where(col < LANES // 2, high, low)
    for i, lanes in enumerate(tiles):
        cot = (gm_ref[:, lanes] * gate_ref[:, lanes].astype(F32)).astype(BF16)
        pairs = dot(spread_groups(x_ref[:, lanes], size), cot, NT)
        for g in range(per):
            lag_parts.append(lag_rows(jnp.where(col >= row, pairs[g * LANES : (g + 1) * LANES], 0.0)))
    lag_ref[...] = lag_sums(lag_parts)


def values_kernel(
    size, modes, local_ref, gate_ref, gm_ref, own_ref, next_ref, table_ref, enter_ref,
    mix_ref, ggl_ref, lag_ref,
):
    per = LANES // size
    row, col = iota((LANES, LANES), 0), iota((LANES, LANES), 1)
    tiles = tiles_of(local_ref)
    mixes, lag_parts = [], []
    for i, lanes in enumerate(tiles):
        table = table_ref[i * LANES : (i + 1) * LANES, :]
        full = local_ref[:, lanes] + carried_part(table, enter_ref, i, modes, size)
        ggl_ref[:, lanes] = (gm_ref[:, lanes] * full).astype(BF16)
        mixes.append((gate_ref[:, lanes].astype(F32) * full).astype(BF16))
    for i, lanes in enumerate(tiles):
        mix_ref[:, lanes] = mixes[i]
        both = jnp.concatenate([own_ref[:, lanes], next_ref[:, lanes]], axis=0)
        pairs = dot(spread_groups(mixes[i], size), both, NT)
        for g in range(per):
            z = pairs[g * LANES : (g + 1) * LANES]
            lag_parts.append(lag_rows(jnp.where(col >= row, z[:, :LANES], z[:, LANES:])))
    lag_ref[...] = lag_sums(lag_parts)


def input_grad_kernel(size, modes, gm_ref, gate_ref, filt_ref, table_ref, enter_ref, out_ref):
    per = LANES // size
    row, col = iota((LANES, LANES), 0), iota((LANES, LANES), 1)
    for i, lanes in enumerate(tiles_of(gm_ref)):
        left = toeplitz(filt_ref, i, per, [col >= row])
        high, low = split(gm_ref[:, lanes] * gate_ref[:, lanes].astype(F32))
        prod = dot(
            jnp.concatenate([left, left[:, :LANES]], axis=1), jnp.concatenate([high, high, low], axis=0)
        )
        table = table_ref[i * LANES : (i + 1) * LANES, :]
        carried = carried_part(table, enter_ref, i, modes, size)
        out_ref[:, lanes] = (pick_groups(prod, LANES, size) + carried).astype(BF16)


def mixer_kernel(size, own_ref, before_ref, taps_ref, cot_ref, out_ref):
    per = LANES // size
    row, col = iota((LANES, LANES), 0), iota((LANES, LANES), 1)
    for i, lanes in enumerate(tiles_of(own_ref)):
        own, before = own_ref[:, lanes], before_ref[:, lanes]
        left = toeplitz(taps_ref, i, per, [col <= row, col > row])
        prod = dot(left, jnp.concatenate([own, before, own, before], axis=0))
        mixed = pick_groups(prod, LANES, size)
        out_ref[:, lanes] = (cot_ref[:, lanes].astype(F32) * mixed).astype(BF16)


def exact_dot(left, right, dims=NN):
    return lax.dot_general(
        left, right, dims, precision=lax.Precision.HIGHEST, preferred_element_type=F32
    )


def prepare_kernel(
    size, own_rows, me_ref, rates_ref, weight_ref, taps_ref, filt_ref, filt_back_ref, taps_back_ref,
    decay_ref, lam_ref,
):
    me = me_ref[0, 0]
    rates, taps = rates_ref[...], taps_ref[...]
    groups, modes = rates.shape
    lag = iota((groups, LANES), 1).astype(F32)
    filt = jnp.zeros((groups, LANES), F32)
    for m in range(modes):
        filt = filt + weight_ref[:, m : m + 1] * jnp.exp(-rates[:, m : m + 1] * lag)
    row, col = iota((LANES, LANES), 0), iota((LANES, LANES), 1)
    mirror = ((row + col) % LANES == 0).astype(F32)
    filt_ref[...] = filt
    filt_back_ref[...] = exact_dot(filt, mirror)
    taps_back_ref[...] = exact_dot(taps, mirror)
    per, parts = LANES // size, modes // own_rows
    pick = iota((8, modes), 1) == me % parts * own_rows + iota((8, modes), 0)
    chosen = exact_dot(pick.astype(F32), rates, NT)
    spread = iota((groups, LANES), 0) == me // parts * per + iota((groups, LANES), 1) // size
    decay_ref[...] = jnp.exp(-exact_dot(chosen, spread.astype(F32))[:own_rows] * LANES)
    own = (iota((groups, LANES), 0) == me).astype(F32)
    lam_ref[...] = jnp.exp(-exact_dot(rates, own, TN) * iota((modes, LANES), 1).astype(F32))


def scan_kernel(x_ref, decay_ref, beside_ref, out_ref):
    decay = decay_ref[...]
    state = jnp.zeros_like(decay)
    for d in range(x_ref.shape[0]):
        out_ref[d] = jnp.concatenate([state, beside_ref[d]], axis=0).astype(BF16)
        state = decay * state + x_ref[d]


def back_scan_kernel(x_ref, decay_ref, front_ref, tap_ref, cot_ref, out_ref, sum_ref):
    decay = decay_ref[...]
    rows = decay.shape[0]
    per = tap_ref.shape[0] // x_ref.shape[0]
    state = jnp.zeros_like(decay)
    total = jnp.zeros_like(decay)
    for d in reversed(range(x_ref.shape[0])):
        x = x_ref[d].astype(F32)[rows:]
        lags = jnp.concatenate(
            [tap_ref[d * per : (d + 1) * per, :], cot_ref[d * per : (d + 1) * per, :]], axis=0
        )
        low = lags - lags.astype(BF16).astype(F32)
        out_ref[d] = jnp.concatenate([state, lags, low], axis=0).astype(BF16)
        state = decay * state + x
        total = total + x * front_ref[d].astype(F32)[:rows]
    sum_ref[...] = total


def collect_kernel(size, x_ref, sum_ref, lam_ref, out_ref):
    rows, modes = sum_ref.shape[0], lam_ref.shape[0]
    lags = jnp.sum(x_ref[...].astype(F32), axis=0)[rows:]
    lags = lags[:2] + lags[2:]
    lam = jnp.concatenate([lam_ref[...], jnp.zeros((LANES - modes, LANES), F32)], axis=0)
    second = exact_dot(jnp.broadcast_to(lags[1:2], (8, LANES)), lam, NT)[:1]
    lane, place = iota((LANES, LANES), 0), iota((LANES, LANES), 1)
    for q in range(rows):
        pick = (place == modes + lane // size * rows + q).astype(F32)
        second = second + exact_dot(jnp.broadcast_to(sum_ref[q : q + 1, :], (8, LANES)), pick, NN)[:1]
    message = jnp.concatenate([lags[:1], second], axis=0)
    out_ref[...] = jnp.broadcast_to(message[None], out_ref.shape)


def finish_kernel(scale, per, rows, x_ref, norm_ref, res_ref, tap_ref):
    modes, count = norm_ref.shape
    x = x_ref[:count]
    for k in range(count, x_ref.shape[0], count):
        x = x + x_ref[k : k + count]
    tap_ref[...] = x[:, 0, :] * scale
    rest = x[:, 1, :]
    total = rest
    h, j = iota(rest.shape, 0) % per, iota(rest.shape, 1) // rows
    for delta in range(1 - per, per):
        moved = rest if delta == 0 else pltpu.roll(rest, delta % count, 0)
        moved = pltpu.roll(moved, (-modes - rows * delta) % LANES, 1)
        total = total + jnp.where(h - j == delta, moved, 0.0)
    res_ref[...] = total.T[:modes] * norm_ref[...] * scale


def call(body, width, step, chunk, specs, outs, args, micros, room=60):
    kinds = list(specs) + [rows for rows, kind in outs]
    chunks = step // chunk

    def kernel(*refs):
        def part(c, carry):
            views = []
            for ref, rows in zip(refs, kinds):
                if rows is None:
                    views.append(ref.at[:, pl.ds(pl.multiple_of(c * chunk, chunk), chunk)])
                else:
                    views.append(ref.at[pl.ds(pl.multiple_of(c * rows, rows), rows), :])
            body(*views)
            return carry

        lax.fori_loop(0, chunks, part, 0)

    def block(rows):
        if rows is None:
            return pl.BlockSpec((LANES, step), lambda i: (0, i))
        return pl.BlockSpec((rows * chunks, LANES), lambda i: (i, 0))

    def shape(rows, kind):
        if rows is None:
            return jax.ShapeDtypeStruct((LANES, width), kind)
        return jax.ShapeDtypeStruct((rows * (width // chunk), LANES), kind)

    nbytes = sum(a.size * a.dtype.itemsize for a in args)
    return pl.pallas_call(
        kernel,
        grid=(width // step,),
        in_specs=[block(rows) for rows in specs],
        out_specs=[block(rows) for rows, kind in outs],
        out_shape=[shape(rows, kind) for rows, kind in outs],
        compiler_params=pltpu.CompilerParams(vmem_limit_bytes=room * 1024 * 1024),
        cost_estimate=pl.CostEstimate(flops=micros * 1_000_000_000, bytes_accessed=nbytes, transcendentals=0),
    )(*args)


def whole(body, outs, args, room=8):
    return pl.pallas_call(
        body,
        out_shape=[jax.ShapeDtypeStruct(shape, kind) for shape, kind in outs],
        compiler_params=pltpu.CompilerParams(vmem_limit_bytes=room * 1024 * 1024),
        cost_estimate=pl.CostEstimate(flops=2_000_000_000, bytes_accessed=1 << 20, transcendentals=0),
    )(*args)


def shifted(x, by):
    count = lax.axis_size("ctx")
    return lax.ppermute(x, "ctx", [(i, i + by) for i in range(count) if 0 <= i + by < count])


def exchange(x, axes="ctx"):
    return lax.all_to_all(x, axes, split_axis=0, concat_axis=0, tiled=True)


def on_device(inputs, gate_li, gate_mr, cotangent, residues, rates, taps):
    seq, gate, cot = inputs[0], gate_li[0], cotangent[0]
    width = seq.shape[1]
    groups, modes = rates.shape
    size = width // groups
    per = LANES // size
    tiles = width // LANES
    reps, count = lax.axis_size("rep"), lax.axis_size("ctx")
    me = lax.axis_index("ctx")
    own_rows = tiles * modes // count
    step = chunk = min(2048, width)
    state_rows = chunk // LANES * modes
    table_rows = per * state_rows
    group_rows = chunk // size
    carry_rows, tile_rows = chunk, chunk // LANES

    scaled = (cot.astype(F32) * gate_mr[0].astype(F32)).astype(BF16)
    after = shifted(scaled, -1)

    lags = jnp.arange(LANES).astype(F32)
    norm = jnp.sqrt(-jnp.expm1(-2.0 * rates))
    weight = residues * norm
    rate3, weight3 = rates[:, :, None], weight[:, :, None]
    to_end = jnp.exp(-rate3 * (LANES - 1.0 - lags))
    from_start = jnp.exp(-rate3 * (lags + 1.0))
    flat = (groups * modes, LANES)
    end_table = to_end.reshape(flat)
    start_table = from_start.reshape(flat)
    rate_row = rates.reshape(tiles, per * modes)
    rate_row = jnp.concatenate([rate_row, rate_row], axis=1)
    weight_row = weight.reshape(tiles, per * modes)
    weight_row = jnp.concatenate([weight_row, weight_row], axis=1)
    filt, filt_back, taps_back, decay, lam_own = pl.pallas_call(
        functools.partial(prepare_kernel, size, own_rows),
        in_specs=[pl.BlockSpec(memory_space=pltpu.SMEM)] + [pl.BlockSpec(memory_space=pltpu.VMEM)] * 3,
        out_shape=[
            jax.ShapeDtypeStruct(shape, F32)
            for shape in (taps.shape, taps.shape, taps.shape, (own_rows, LANES), (modes, LANES))
        ],
        compiler_params=pltpu.CompilerParams(vmem_limit_bytes=60 * 1024 * 1024),
        cost_estimate=pl.CostEstimate(flops=3_000_000_000, bytes_accessed=1 << 20, transcendentals=0),
    )(me.astype(jnp.int32).reshape(1, 1), rates, weight, taps)

    bind = functools.partial
    states = call(
        bind(states_kernel, size, modes), width, step, chunk, [None, table_rows], [(state_rows, F32)],
        [seq, end_table], 3,
    )[0]
    ends = exchange(states.reshape(count, own_rows, LANES))

    after, filt, filt_back, taps_back, decay, lam_own = lax.optimization_barrier(
        (after, filt, filt_back, taps_back, decay, lam_own)
    )
    grad_mixer, back_states = call(
        bind(mixer_back_kernel, size, modes), width, step, chunk,
        [None, None, None, group_rows, table_rows], [(None, F32), (state_rows, F32)],
        [scaled, after, gate, taps, start_table], 8,
    )
    first = whole(
        scan_kernel, [((count, 2 * own_rows, LANES), BF16)],
        [ends, decay, back_states.reshape(count, own_rows, LANES)],
    )[0]
    second = exchange(first)
    local, front_table, back_table, lag_cot = call(
        bind(local_kernel, size), width, step, chunk,
        [None, None, None, group_rows, tile_rows, tile_rows],
        [(None, F32), (carry_rows, BF16), (carry_rows, BF16), (group_rows, F32)],
        [seq, gate, grad_mixer, filt_back, rate_row, weight_row], 10,
    )
    mixer_in, grad_gate_li, lag_taps = call(
        bind(values_kernel, size, modes), width, step, chunk,
        [None, None, None, None, None, carry_rows, 2 * state_rows],
        [(None, BF16), (None, BF16), (group_rows, F32)],
        [local, gate, grad_mixer, scaled, after, front_table, second.reshape(-1, LANES)], 6,
    )
    before = shifted(mixer_in, 1)
    message, state_sums = whole(
        back_scan_kernel, [(first.shape, BF16), (decay.shape, F32)],
        [second, decay, first, lag_taps, lag_cot], 60,
    )
    third = exchange(message)
    grad_gate_mr = call(
        bind(mixer_kernel, size), width, step, chunk, [None, None, group_rows, None], [(None, BF16)],
        [mixer_in, before, taps_back, cot], 7, 32,
    )[0]
    third, grad_gate_mr = lax.optimization_barrier((third, grad_gate_mr))
    spread = whole(
        bind(collect_kernel, size), [((reps * count, 2, LANES), F32)], [third, state_sums, lam_own]
    )[0]
    got = exchange(spread, ("rep", "ctx"))
    grad_inputs = call(
        bind(input_grad_kernel, size, modes), width, step, chunk,
        [None, None, group_rows, carry_rows, 2 * state_rows], [(None, BF16)],
        [grad_mixer, gate, filt, back_table, third.reshape(-1, LANES)], 7,
    )[0]
    grad_residues, grad_taps = whole(
        bind(finish_kernel, 1.0 / math.sqrt(reps * count * LANES), per, own_rows),
        [((modes, groups), F32), (taps.shape, F32)], [got, norm.T],
    )
    return grad_inputs[None], grad_gate_li[None], grad_gate_mr[None], grad_residues.T, grad_taps


def solution(mesh):
    big = P("rep", "ctx", None)
    return jax.shard_map(
        on_device,
        mesh=mesh,
        in_specs=(big, big, big, big, P(), P(), P()),
        out_specs=(big, big, big, P(), P()),
        check_vma=False,
    )
```

```python
import functools
import math

import jax
import jax.numpy as jnp
from jax import lax
from jax.experimental import pallas as pl
from jax.experimental.pallas import tpu as pltpu
from jax.sharding import PartitionSpec as P

F32 = jnp.float32
BF16 = jnp.bfloat16
LANES = 128
NN = (((1,), (0,)), ((), ()))
NT = (((1,), (1,)), ((), ()))
TN = (((0,), (0,)), ((), ()))


def dot(left, right, dims=NN):
    return lax.dot_general(left, right, dims, preferred_element_type=F32)


def split(x):
    high = x.astype(BF16)
    return high, (x - high.astype(F32)).astype(BF16)


def iota(shape, dim):
    return lax.broadcasted_iota(jnp.int32, shape, dim)


def roll_left(x, amount):
    return pltpu.roll(x, x.shape[1] - amount, 1)


def pick_groups(stacked, rows, size):
    lane_group = iota((rows, LANES), 1) // size
    out = stacked[:rows]
    for g in range(1, LANES // size):
        out = jnp.where(lane_group == g, stacked[g * rows : (g + 1) * rows], out)
    return out


def spread_groups(x, size):
    lane_group = iota(x.shape, 1) // size
    zero = jnp.zeros_like(x)
    return jnp.concatenate(
        [jnp.where(lane_group == g, x, zero) for g in range(LANES // size)], axis=0
    )


def circulant(row):
    return split(pltpu.roll(jnp.broadcast_to(row, (LANES, LANES)), 0, 1, stride=1, stride_axis=0))


def masked(row, keeps):
    parts = circulant(row)
    zero = jnp.zeros_like(parts[0])
    return jnp.concatenate([jnp.where(keep, part, zero) for part in parts for keep in keeps], axis=1)


def toeplitz(rows_ref, i, per, keeps):
    return jnp.concatenate(
        [masked(rows_ref[i * per + g : i * per + g + 1, :], keeps) for g in range(per)], axis=0
    )


def lag_rows(z):
    sums = [None] * 4
    for k in range(LANES // 8):
        part = z[8 * k : 8 * k + 8]
        part = roll_left(part, 8 * k) if k else part
        sums[k % 4] = part if sums[k % 4] is None else sums[k % 4] + part
    return (sums[0] + sums[1]) + (sums[2] + sums[3])


def lag_sums(rows):
    rows = jnp.concatenate(rows, axis=0)
    sub = iota(rows.shape, 0)
    for bit in (4, 2, 1):
        rows = jnp.where((sub & bit) != 0, roll_left(rows, bit), rows)
    return jnp.sum(rows.reshape(-1, 8, LANES), axis=1)


def carried_part(table, ref, i, modes, size):
    x = ref[i * 2 * modes : (i + 1) * 2 * modes, :].astype(F32)
    x = jnp.concatenate([x[k : k + 4] for k in range(0, 2 * modes, 8)], axis=0)
    x = spread_groups(x, size).astype(BF16)
    return dot(table, jnp.concatenate([x, x], axis=0))


def mode_sums(table, x, size, modes):
    high, low = split(table)
    if x.dtype == BF16:
        prod = dot(jnp.concatenate([high, low], axis=0), x)
    else:
        left = jnp.concatenate(
            [jnp.concatenate([high, high], axis=1), jnp.concatenate([low, low], axis=1)], axis=0
        )
        prod = dot(left, jnp.concatenate(split(x), axis=0))
    half = prod.shape[0] // 2
    return pick_groups(prod[:half] + prod[half:], modes, size)


def tiles_of(ref):
    return [slice(i * LANES, (i + 1) * LANES) for i in range(ref.shape[1] // LANES)]


def states_kernel(size, modes, x_ref, rate_ref, out_ref):
    rows = LANES // size * modes
    steps = LANES - 1.0 - iota((rows, LANES), 1).astype(F32)
    out = [
        mode_sums(jnp.exp(-rate_ref[i * rows : (i + 1) * rows, :] * steps), x_ref[:, lanes], size, modes)
        for i, lanes in enumerate(tiles_of(x_ref))
    ]
    out_ref[...] = jnp.concatenate(out, axis=0)


def mixer_back_kernel(size, modes, own_ref, next_ref, gate_ref, taps_ref, rate_ref, gm_ref, out_ref):
    per = LANES // size
    rows = per * modes
    row, col = iota((LANES, LANES), 0), iota((LANES, LANES), 1)
    tiles = tiles_of(own_ref)
    cots, out = [], []
    for i, lanes in enumerate(tiles):
        own, after = own_ref[:, lanes], next_ref[:, lanes]
        left = toeplitz(taps_ref, i, per, [col >= row, col < row])
        prod = dot(left, jnp.concatenate([own, after, own, after], axis=0))
        grad_mixer = pick_groups(prod, LANES, size)
        gm_ref[:, lanes] = grad_mixer
        cots.append(grad_mixer * gate_ref[:, lanes].astype(F32))
    steps = iota((rows, LANES), 1).astype(F32) + 1.0
    for i, lanes in enumerate(tiles):
        table = jnp.exp(-rate_ref[i * rows : (i + 1) * rows, :] * steps)
        out.append(mode_sums(table, cots[i], size, modes))
    out_ref[...] = jnp.concatenate(out, axis=0)


def local_kernel(
    size, x_ref, gate_ref, gm_ref, filt_ref, rate_ref, weight_ref,
    out_ref, front_ref, back_ref, lag_ref,
):
    per = LANES // size
    row, col = iota((LANES, LANES), 0), iota((LANES, LANES), 1)
    up = row.astype(F32)
    tiles = tiles_of(x_ref)
    lag_parts = []
    for i, lanes in enumerate(tiles):
        x = x_ref[:, lanes]
        prod = dot(toeplitz(filt_ref, i, per, [col <= row]), jnp.concatenate([x, x], axis=0))
        out_ref[:, lanes] = pick_groups(prod, LANES, size)
    for i in range(len(tiles)):
        rate, weight = rate_ref[i : i + 1, :], weight_ref[i : i + 1, :]
        for ref, steps in ((front_ref, up + 1.0), (back_ref, LANES - 1.0 - up)):
            high, low = split(weight * jnp.exp(-rate * steps))
            ref[i * LANES : (i + 1) * LANES, :] = jnp.where(col < LANES // 2, high, low)
    for i, lanes in enumerate(tiles):
        cot = (gm_ref[:, lanes] * gate_ref[:, lanes].astype(F32)).astype(BF16)
        pairs = dot(spread_groups(x_ref[:, lanes], size), cot, NT)
        for g in range(per):
            lag_parts.append(lag_rows(jnp.where(col >= row, pairs[g * LANES : (g + 1) * LANES], 0.0)))
    lag_ref[...] = lag_sums(lag_parts)


def values_kernel(
    size, modes, local_ref, gate_ref, own_ref, next_ref, table_ref, enter_ref, mix_ref, lag_ref
):
    per = LANES // size
    row, col = iota((LANES, LANES), 0), iota((LANES, LANES), 1)
    tiles = tiles_of(local_ref)
    mixes, lag_parts = [], []
    for i, lanes in enumerate(tiles):
        table = table_ref[i * LANES : (i + 1) * LANES, :]
        full = local_ref[:, lanes] + carried_part(table, enter_ref, i, modes, size)
        mixes.append((gate_ref[:, lanes].astype(F32) * full).astype(BF16))
    for i, lanes in enumerate(tiles):
        mix_ref[:, lanes] = mixes[i]
        both = jnp.concatenate([own_ref[:, lanes], next_ref[:, lanes]], axis=0)
        pairs = dot(spread_groups(mixes[i], size), both, NT)
        for g in range(per):
            z = pairs[g * LANES : (g + 1) * LANES]
            lag_parts.append(lag_rows(jnp.where(col >= row, z[:, :LANES], z[:, LANES:])))
    lag_ref[...] = lag_sums(lag_parts)


def gate_grad_kernel(size, modes, local_ref, gm_ref, table_ref, enter_ref, out_ref):
    for i, lanes in enumerate(tiles_of(local_ref)):
        table = table_ref[i * LANES : (i + 1) * LANES, :]
        full = local_ref[:, lanes] + carried_part(table, enter_ref, i, modes, size)
        out_ref[:, lanes] = (gm_ref[:, lanes] * full).astype(BF16)


def input_grad_kernel(size, modes, gm_ref, gate_ref, filt_ref, table_ref, enter_ref, out_ref):
    per = LANES // size
    row, col = iota((LANES, LANES), 0), iota((LANES, LANES), 1)
    for i, lanes in enumerate(tiles_of(gm_ref)):
        left = toeplitz(filt_ref, i, per, [col >= row])
        high, low = split(gm_ref[:, lanes] * gate_ref[:, lanes].astype(F32))
        prod = dot(
            jnp.concatenate([left, left[:, :LANES]], axis=1), jnp.concatenate([high, high, low], axis=0)
        )
        table = table_ref[i * LANES : (i + 1) * LANES, :]
        carried = carried_part(table, enter_ref, i, modes, size)
        out_ref[:, lanes] = (pick_groups(prod, LANES, size) + carried).astype(BF16)


def mixer_kernel(size, own_ref, before_ref, taps_ref, cot_ref, out_ref):
    per = LANES // size
    row, col = iota((LANES, LANES), 0), iota((LANES, LANES), 1)
    for i, lanes in enumerate(tiles_of(own_ref)):
        own, before = own_ref[:, lanes], before_ref[:, lanes]
        left = toeplitz(taps_ref, i, per, [col <= row, col > row])
        prod = dot(left, jnp.concatenate([own, before, own, before], axis=0))
        mixed = pick_groups(prod, LANES, size)
        out_ref[:, lanes] = (cot_ref[:, lanes].astype(F32) * mixed).astype(BF16)


def exact_dot(left, right, dims=NN):
    return lax.dot_general(
        left, right, dims, precision=lax.Precision.HIGHEST, preferred_element_type=F32
    )


def filters_kernel(rates_ref, weight_ref, taps_ref, filt_ref, filt_back_ref, taps_back_ref):
    rates, taps = rates_ref[...], taps_ref[...]
    groups, modes = rates.shape
    lag = iota((groups, LANES), 1).astype(F32)
    filt = jnp.zeros((groups, LANES), F32)
    for m in range(modes):
        filt = filt + weight_ref[:, m : m + 1] * jnp.exp(-rates[:, m : m + 1] * lag)
    mirror = ((iota((LANES, LANES), 0) + iota((LANES, LANES), 1)) % LANES == 0).astype(F32)
    filt_ref[...] = filt
    filt_back_ref[...] = exact_dot(filt, mirror)
    taps_back_ref[...] = exact_dot(taps, mirror)


def owner_kernel(size, own_rows, me_ref, rates_ref, decay_ref, lam_ref):
    me = me_ref[0, 0]
    rates = rates_ref[...]
    groups, modes = rates.shape
    per, parts = LANES // size, modes // own_rows
    pick = iota((8, modes), 1) == me % parts * own_rows + iota((8, modes), 0)
    chosen = exact_dot(pick.astype(F32), rates, NT)
    spread = iota((groups, LANES), 0) == me // parts * per + iota((groups, LANES), 1) // size
    decay_ref[...] = jnp.exp(-exact_dot(chosen, spread.astype(F32))[:own_rows] * LANES)
    own = (iota((groups, LANES), 0) == me).astype(F32)
    lam_ref[...] = jnp.exp(-exact_dot(rates, own, TN) * iota((modes, LANES), 1).astype(F32))


def scan_kernel(x_ref, decay_ref, beside_ref, out_ref):
    decay = decay_ref[...]
    state = jnp.zeros_like(decay)
    for d in range(x_ref.shape[0]):
        out_ref[d] = jnp.concatenate([state, beside_ref[d]], axis=0).astype(BF16)
        state = decay * state + x_ref[d]


def back_scan_kernel(x_ref, decay_ref, front_ref, tap_ref, cot_ref, out_ref, sum_ref):
    decay = decay_ref[...]
    rows = decay.shape[0]
    per = tap_ref.shape[0] // x_ref.shape[0]
    state = jnp.zeros_like(decay)
    total = jnp.zeros_like(decay)
    for d in reversed(range(x_ref.shape[0])):
        x = x_ref[d].astype(F32)[rows:]
        lags = jnp.concatenate(
            [tap_ref[d * per : (d + 1) * per, :], cot_ref[d * per : (d + 1) * per, :]], axis=0
        )
        low = lags - lags.astype(BF16).astype(F32)
        out_ref[d] = jnp.concatenate([state, lags, low], axis=0).astype(BF16)
        state = decay * state + x
        total = total + x * front_ref[d].astype(F32)[:rows]
    sum_ref[...] = total


def collect_kernel(size, x_ref, sum_ref, lam_ref, out_ref):
    rows, modes = sum_ref.shape[0], lam_ref.shape[0]
    lags = jnp.sum(x_ref[...].astype(F32), axis=0)[rows:]
    lags = lags[:2] + lags[2:]
    lam = jnp.concatenate([lam_ref[...], jnp.zeros((LANES - modes, LANES), F32)], axis=0)
    second = exact_dot(jnp.broadcast_to(lags[1:2], (8, LANES)), lam, NT)[:1]
    lane, place = iota((LANES, LANES), 0), iota((LANES, LANES), 1)
    for q in range(rows):
        pick = (place == modes + lane // size * rows + q).astype(F32)
        second = second + exact_dot(jnp.broadcast_to(sum_ref[q : q + 1, :], (8, LANES)), pick, NN)[:1]
    message = jnp.concatenate([lags[:1], second], axis=0)
    out_ref[...] = jnp.broadcast_to(message[None], out_ref.shape)


def finish_kernel(scale, per, rows, x_ref, norm_ref, res_ref, tap_ref):
    modes, count = norm_ref.shape
    x = x_ref[:count]
    for k in range(count, x_ref.shape[0], count):
        x = x + x_ref[k : k + count]
    tap_ref[...] = x[:, 0, :] * scale
    rest = x[:, 1, :]
    total = rest
    h, j = iota(rest.shape, 0) % per, iota(rest.shape, 1) // rows
    for delta in range(1 - per, per):
        moved = rest if delta == 0 else pltpu.roll(rest, delta % count, 0)
        moved = pltpu.roll(moved, (-modes - rows * delta) % LANES, 1)
        total = total + jnp.where(h - j == delta, moved, 0.0)
    res_ref[...] = total.T[:modes] * norm_ref[...] * scale


def call(body, width, step, chunk, specs, outs, args, micros, room=60):
    kinds = list(specs) + [rows for rows, kind in outs]
    chunks = step // chunk

    def kernel(*refs):
        def part(c, carry):
            views = []
            for ref, rows in zip(refs, kinds):
                if rows is None:
                    views.append(ref.at[:, pl.ds(pl.multiple_of(c * chunk, chunk), chunk)])
                else:
                    views.append(ref.at[pl.ds(pl.multiple_of(c * rows, rows), rows), :])
            body(*views)
            return carry

        lax.fori_loop(0, chunks, part, 0)

    def block(rows):
        if rows is None:
            return pl.BlockSpec((LANES, step), lambda i: (0, i))
        return pl.BlockSpec((rows * chunks, LANES), lambda i: (i, 0))

    def shape(rows, kind):
        if rows is None:
            return jax.ShapeDtypeStruct((LANES, width), kind)
        return jax.ShapeDtypeStruct((rows * (width // chunk), LANES), kind)

    nbytes = sum(a.size * a.dtype.itemsize for a in args)
    return pl.pallas_call(
        kernel,
        grid=(width // step,),
        in_specs=[block(rows) for rows in specs],
        out_specs=[block(rows) for rows, kind in outs],
        out_shape=[shape(rows, kind) for rows, kind in outs],
        compiler_params=pltpu.CompilerParams(vmem_limit_bytes=room * 1024 * 1024),
        cost_estimate=pl.CostEstimate(flops=micros * 1_000_000_000, bytes_accessed=nbytes, transcendentals=0),
    )(*args)


def whole(body, outs, args, room=8):
    return pl.pallas_call(
        body,
        out_shape=[jax.ShapeDtypeStruct(shape, kind) for shape, kind in outs],
        compiler_params=pltpu.CompilerParams(vmem_limit_bytes=room * 1024 * 1024),
        cost_estimate=pl.CostEstimate(flops=2_000_000_000, bytes_accessed=1 << 20, transcendentals=0),
    )(*args)


def shifted(x, by):
    count = lax.axis_size("ctx")
    return lax.ppermute(x, "ctx", [(i, i + by) for i in range(count) if 0 <= i + by < count])


def exchange(x, axes="ctx"):
    return lax.all_to_all(x, axes, split_axis=0, concat_axis=0, tiled=True)


def on_device(inputs, gate_li, gate_mr, cotangent, residues, rates, taps):
    seq, gate, cot = inputs[0], gate_li[0], cotangent[0]
    width = seq.shape[1]
    groups, modes = rates.shape
    size = width // groups
    per = LANES // size
    tiles = width // LANES
    reps, count = lax.axis_size("rep"), lax.axis_size("ctx")
    me = lax.axis_index("ctx")
    own_rows = tiles * modes // count
    step = chunk = min(2048, width)
    state_rows = chunk // LANES * modes
    table_rows = per * state_rows
    group_rows = chunk // size
    carry_rows, tile_rows = chunk, chunk // LANES

    scaled = (cot.astype(F32) * gate_mr[0].astype(F32)).astype(BF16)
    after = shifted(scaled, -1)

    norm = jnp.sqrt(-jnp.expm1(-2.0 * rates))
    weight = residues * norm
    rate_rows = jnp.broadcast_to(rates.reshape(-1, 1), (groups * modes, LANES))
    rate_row = rates.reshape(tiles, per * modes)
    rate_row = jnp.concatenate([rate_row, rate_row], axis=1)
    weight_row = weight.reshape(tiles, per * modes)
    weight_row = jnp.concatenate([weight_row, weight_row], axis=1)
    decay, lam_own = pl.pallas_call(
        functools.partial(owner_kernel, size, own_rows),
        in_specs=[pl.BlockSpec(memory_space=pltpu.SMEM), pl.BlockSpec(memory_space=pltpu.VMEM)],
        out_shape=[
            jax.ShapeDtypeStruct((own_rows, LANES), F32), jax.ShapeDtypeStruct((modes, LANES), F32)
        ],
        compiler_params=pltpu.CompilerParams(vmem_limit_bytes=8 * 1024 * 1024),
        cost_estimate=pl.CostEstimate(flops=1_000_000_000, bytes_accessed=1 << 16, transcendentals=0),
    )(me.astype(jnp.int32).reshape(1, 1), rates)
    bind = functools.partial
    states = call(
        bind(states_kernel, size, modes), width, step, chunk, [None, table_rows], [(state_rows, F32)],
        [seq, rate_rows], 3,
    )[0]
    ends = exchange(states.reshape(count, own_rows, LANES))

    after, decay, lam_own = lax.optimization_barrier((after, decay, lam_own))
    grad_mixer, back_states = call(
        bind(mixer_back_kernel, size, modes), width, step, chunk,
        [None, None, None, group_rows, table_rows], [(None, F32), (state_rows, F32)],
        [scaled, after, gate, taps, rate_rows], 8,
    )
    first = whole(
        scan_kernel, [((count, 2 * own_rows, LANES), BF16)],
        [ends, decay, back_states.reshape(count, own_rows, LANES)],
    )[0]
    second = exchange(first)
    late = lax.optimization_barrier((rates, weight, taps, first))[:3]
    filt, filt_back, taps_back = whole(filters_kernel, [(taps.shape, F32)] * 3, late, 60)
    local, front_table, back_table, lag_cot = call(
        bind(local_kernel, size), width, step, chunk,
        [None, None, None, group_rows, tile_rows, tile_rows],
        [(None, F32), (carry_rows, BF16), (carry_rows, BF16), (group_rows, F32)],
        [seq, gate, grad_mixer, filt_back, rate_row, weight_row], 10,
    )
    mixer_in, lag_taps = call(
        bind(values_kernel, size, modes), width, step, chunk,
        [None, None, None, None, carry_rows, 2 * state_rows], [(None, BF16), (group_rows, F32)],
        [local, gate, scaled, after, front_table, second.reshape(-1, LANES)], 6,
    )
    before = shifted(mixer_in, 1)
    message, state_sums = whole(
        back_scan_kernel, [(first.shape, BF16), (decay.shape, F32)],
        [second, decay, first, lag_taps, lag_cot], 60,
    )
    third = exchange(message)
    grad_gate_li = call(
        bind(gate_grad_kernel, size, modes), width, step, chunk,
        [None, None, carry_rows, 2 * state_rows], [(None, BF16)],
        [local, grad_mixer, front_table, second.reshape(-1, LANES)], 4,
    )[0]
    grad_gate_mr = call(
        bind(mixer_kernel, size), width, step, chunk, [None, None, group_rows, None], [(None, BF16)],
        [mixer_in, before, taps_back, cot], 7, 32,
    )[0]
    spread = whole(
        bind(collect_kernel, size), [((reps * count, 2, LANES), F32)], [third, state_sums, lam_own]
    )[0]
    got = exchange(spread, ("rep", "ctx"))
    grad_inputs = call(
        bind(input_grad_kernel, size, modes), width, step, chunk,
        [None, None, group_rows, carry_rows, 2 * state_rows], [(None, BF16)],
        [grad_mixer, gate, filt, back_table, third.reshape(-1, LANES)], 7,
    )[0]
    got, grad_gate_mr = lax.optimization_barrier((got, grad_gate_mr))
    grad_residues, grad_taps = whole(
        bind(finish_kernel, 1.0 / math.sqrt(reps * count * LANES), per, own_rows),
        [((modes, groups), F32), (taps.shape, F32)], [got, norm.T],
    )
    return grad_inputs[None], grad_gate_li[None], grad_gate_mr[None], grad_residues.T, grad_taps


def solution(mesh):
    big = P("rep", "ctx", None)
    return jax.shard_map(
        on_device,
        mesh=mesh,
        in_specs=(big, big, big, big, P(), P(), P()),
        out_specs=(big, big, big, P(), P()),
        check_vma=False,
    )
```

```python
import functools
import math

import jax
import jax.numpy as jnp
from jax import lax
from jax.experimental import pallas as pl
from jax.experimental.pallas import tpu as pltpu
from jax.sharding import PartitionSpec as P

F32 = jnp.float32
BF16 = jnp.bfloat16
LANES = 128
NN = (((1,), (0,)), ((), ()))
NT = (((1,), (1,)), ((), ()))
TN = (((0,), (0,)), ((), ()))


def dot(left, right, dims=NN):
    return lax.dot_general(left, right, dims, preferred_element_type=F32)


def split(x):
    high = x.astype(BF16)
    return high, (x - high.astype(F32)).astype(BF16)


def iota(shape, dim):
    return lax.broadcasted_iota(jnp.int32, shape, dim)


def roll_left(x, amount):
    return pltpu.roll(x, x.shape[1] - amount, 1)


def pick_groups(stacked, rows, size):
    lane_group = iota((rows, LANES), 1) // size
    out = stacked[:rows]
    for g in range(1, LANES // size):
        out = jnp.where(lane_group == g, stacked[g * rows : (g + 1) * rows], out)
    return out


def spread_groups(x, size):
    lane_group = iota(x.shape, 1) // size
    zero = jnp.zeros_like(x)
    return jnp.concatenate(
        [jnp.where(lane_group == g, x, zero) for g in range(LANES // size)], axis=0
    )


def circulant(row):
    return split(pltpu.roll(jnp.broadcast_to(row, (LANES, LANES)), 0, 1, stride=1, stride_axis=0))


def masked(row, keeps):
    parts = circulant(row)
    zero = jnp.zeros_like(parts[0])
    return jnp.concatenate([jnp.where(keep, part, zero) for part in parts for keep in keeps], axis=1)


def toeplitz(rows_ref, i, per, keeps):
    return jnp.concatenate(
        [masked(rows_ref[i * per + g : i * per + g + 1, :], keeps) for g in range(per)], axis=0
    )


def lag_rows(z):
    sums = [None] * 4
    for k in range(LANES // 8):
        part = z[8 * k : 8 * k + 8]
        part = roll_left(part, 8 * k) if k else part
        sums[k % 4] = part if sums[k % 4] is None else sums[k % 4] + part
    return (sums[0] + sums[1]) + (sums[2] + sums[3])


def lag_sums(rows):
    rows = jnp.concatenate(rows, axis=0)
    sub = iota(rows.shape, 0)
    for bit in (4, 2, 1):
        rows = jnp.where((sub & bit) != 0, roll_left(rows, bit), rows)
    return jnp.sum(rows.reshape(-1, 8, LANES), axis=1)


def carry_table(rate_ref, weight_ref, i, steps):
    high, low = split(weight_ref[i : i + 1, :] * jnp.exp(-rate_ref[i : i + 1, :] * steps))
    return jnp.where(iota(steps.shape, 1) < LANES // 2, high, low)


def carried_part(table, ref, i, modes, size):
    x = ref[i * 2 * modes : (i + 1) * 2 * modes, :].astype(F32)
    x = jnp.concatenate([x[k : k + 4] for k in range(0, 2 * modes, 8)], axis=0)
    x = spread_groups(x, size).astype(BF16)
    return dot(table, jnp.concatenate([x, x], axis=0))


def mode_sums(table, x, size, modes):
    high, low = split(table)
    if x.dtype == BF16:
        prod = dot(jnp.concatenate([high, low], axis=0), x)
    else:
        left = jnp.concatenate(
            [jnp.concatenate([high, high], axis=1), jnp.concatenate([low, low], axis=1)], axis=0
        )
        prod = dot(left, jnp.concatenate(split(x), axis=0))
    half = prod.shape[0] // 2
    return pick_groups(prod[:half] + prod[half:], modes, size)


def tiles_of(ref):
    return [slice(i * LANES, (i + 1) * LANES) for i in range(ref.shape[1] // LANES)]


def states_kernel(size, modes, x_ref, rate_ref, out_ref):
    rows = LANES // size * modes
    steps = LANES - 1.0 - iota((rows, LANES), 1).astype(F32)
    out = [
        mode_sums(jnp.exp(-rate_ref[i * rows : (i + 1) * rows, :] * steps), x_ref[:, lanes], size, modes)
        for i, lanes in enumerate(tiles_of(x_ref))
    ]
    out_ref[...] = jnp.concatenate(out, axis=0).astype(out_ref.dtype)


def mixer_back_kernel(size, modes, own_ref, next_ref, gate_ref, taps_ref, rate_ref, gm_ref, out_ref):
    per = LANES // size
    rows = per * modes
    row, col = iota((LANES, LANES), 0), iota((LANES, LANES), 1)
    tiles = tiles_of(own_ref)
    cots, out = [], []
    for i, lanes in enumerate(tiles):
        own, after = own_ref[:, lanes], next_ref[:, lanes]
        left = toeplitz(taps_ref, i, per, [col >= row, col < row])
        prod = dot(left, jnp.concatenate([own, after, own, after], axis=0))
        grad_mixer = pick_groups(prod, LANES, size)
        gm_ref[:, lanes] = grad_mixer
        cots.append(grad_mixer * gate_ref[:, lanes].astype(F32))
    steps = iota((rows, LANES), 1).astype(F32) + 1.0
    for i, lanes in enumerate(tiles):
        table = jnp.exp(-rate_ref[i * rows : (i + 1) * rows, :] * steps)
        out.append(mode_sums(table, cots[i], size, modes))
    out_ref[...] = jnp.concatenate(out, axis=0)


def local_kernel(
    size, x_ref, gate_ref, gm_ref, filt_ref, rate_ref, weight_ref, out_ref, table_ref, lag_ref
):
    per = LANES // size
    row, col = iota((LANES, LANES), 0), iota((LANES, LANES), 1)
    up = row.astype(F32)
    tiles = tiles_of(x_ref)
    lag_parts = []
    for i, lanes in enumerate(tiles):
        x = x_ref[:, lanes]
        prod = dot(toeplitz(filt_ref, i, per, [col <= row]), jnp.concatenate([x, x], axis=0))
        out_ref[:, lanes] = pick_groups(prod, LANES, size)
    for i in range(len(tiles)):
        table_ref[i * LANES : (i + 1) * LANES, :] = carry_table(rate_ref, weight_ref, i, up + 1.0)
    for i, lanes in enumerate(tiles):
        cot = (gm_ref[:, lanes] * gate_ref[:, lanes].astype(F32)).astype(BF16)
        pairs = dot(spread_groups(x_ref[:, lanes], size), cot, NT)
        for g in range(per):
            lag_parts.append(lag_rows(jnp.where(col >= row, pairs[g * LANES : (g + 1) * LANES], 0.0)))
    lag_ref[...] = lag_sums(lag_parts)


def values_kernel(
    size, modes, local_ref, gate_ref, own_ref, next_ref, table_ref, enter_ref, mix_ref, lag_ref
):
    per = LANES // size
    row, col = iota((LANES, LANES), 0), iota((LANES, LANES), 1)
    tiles = tiles_of(local_ref)
    mixes, lag_parts = [], []
    for i, lanes in enumerate(tiles):
        table = table_ref[i * LANES : (i + 1) * LANES, :]
        full = local_ref[:, lanes] + carried_part(table, enter_ref, i, modes, size)
        mixes.append((gate_ref[:, lanes].astype(F32) * full).astype(BF16))
    for i, lanes in enumerate(tiles):
        mix_ref[:, lanes] = mixes[i]
        both = jnp.concatenate([own_ref[:, lanes], next_ref[:, lanes]], axis=0)
        pairs = dot(spread_groups(mixes[i], size), both, NT)
        for g in range(per):
            z = pairs[g * LANES : (g + 1) * LANES]
            lag_parts.append(lag_rows(jnp.where(col >= row, z[:, :LANES], z[:, LANES:])))
    lag_ref[...] = lag_sums(lag_parts)


def gate_grad_kernel(size, modes, local_ref, gm_ref, table_ref, enter_ref, out_ref):
    for i, lanes in enumerate(tiles_of(local_ref)):
        table = table_ref[i * LANES : (i + 1) * LANES, :]
        full = local_ref[:, lanes] + carried_part(table, enter_ref, i, modes, size)
        out_ref[:, lanes] = (gm_ref[:, lanes] * full).astype(BF16)


def input_grad_kernel(
    size, modes, gm_ref, gate_ref, filt_ref, rate_ref, weight_ref, enter_ref, out_ref
):
    per = LANES // size
    row, col = iota((LANES, LANES), 0), iota((LANES, LANES), 1)
    for i, lanes in enumerate(tiles_of(gm_ref)):
        left = toeplitz(filt_ref, i, per, [col >= row])
        high, low = split(gm_ref[:, lanes] * gate_ref[:, lanes].astype(F32))
        prod = dot(
            jnp.concatenate([left, left[:, :LANES]], axis=1), jnp.concatenate([high, high, low], axis=0)
        )
        table = carry_table(rate_ref, weight_ref, i, LANES - 1.0 - row.astype(F32))
        carried = carried_part(table, enter_ref, i, modes, size)
        out_ref[:, lanes] = (pick_groups(prod, LANES, size) + carried).astype(BF16)


def mixer_kernel(size, own_ref, before_ref, taps_ref, cot_ref, out_ref):
    per = LANES // size
    row, col = iota((LANES, LANES), 0), iota((LANES, LANES), 1)
    for i, lanes in enumerate(tiles_of(own_ref)):
        own, before = own_ref[:, lanes], before_ref[:, lanes]
        left = toeplitz(taps_ref, i, per, [col <= row, col > row])
        prod = dot(left, jnp.concatenate([own, before, own, before], axis=0))
        mixed = pick_groups(prod, LANES, size)
        out_ref[:, lanes] = (cot_ref[:, lanes].astype(F32) * mixed).astype(BF16)


def exact_dot(left, right, dims=NN):
    return lax.dot_general(
        left, right, dims, precision=lax.Precision.HIGHEST, preferred_element_type=F32
    )


def filters_kernel(rates_ref, weight_ref, taps_ref, filt_ref, filt_back_ref, taps_back_ref):
    rates, weight, taps = rates_ref[...].T, weight_ref[...].T, taps_ref[...]
    groups, modes = rates.shape
    lag = iota((groups, LANES), 1).astype(F32)
    filt = jnp.zeros((groups, LANES), F32)
    for m in range(modes):
        filt = filt + weight[:, m : m + 1] * jnp.exp(-rates[:, m : m + 1] * lag)
    mirror = ((iota((LANES, LANES), 0) + iota((LANES, LANES), 1)) % LANES == 0).astype(F32)
    filt_ref[...] = filt
    filt_back_ref[...] = exact_dot(filt, mirror)
    taps_back_ref[...] = exact_dot(taps, mirror)


def owner_kernel(size, own_rows, me_ref, rates_ref, decay_ref, lam_ref):
    me = me_ref[0, 0]
    rates = rates_ref[...]
    groups, modes = rates.shape
    per, parts = LANES // size, modes // own_rows
    pick = iota((8, modes), 1) == me % parts * own_rows + iota((8, modes), 0)
    chosen = exact_dot(pick.astype(F32), rates, NT)
    spread = iota((groups, LANES), 0) == me // parts * per + iota((groups, LANES), 1) // size
    decay_ref[...] = jnp.exp(-exact_dot(chosen, spread.astype(F32))[:own_rows] * LANES)
    own = (iota((groups, LANES), 0) == me).astype(F32)
    lam_ref[...] = jnp.exp(-exact_dot(rates, own, TN) * iota((modes, LANES), 1).astype(F32))


def scan_kernel(x_ref, decay_ref, beside_ref, out_ref):
    decay = decay_ref[...]
    state = jnp.zeros_like(decay)
    for d in range(x_ref.shape[0]):
        out_ref[d] = jnp.concatenate([state, beside_ref[d]], axis=0).astype(BF16)
        state = decay * state + x_ref[d].astype(F32)


def back_scan_kernel(x_ref, decay_ref, front_ref, tap_ref, cot_ref, out_ref, sum_ref):
    decay = decay_ref[...]
    rows = decay.shape[0]
    per = tap_ref.shape[0] // x_ref.shape[0]
    state = jnp.zeros_like(decay)
    total = jnp.zeros_like(decay)
    for d in reversed(range(x_ref.shape[0])):
        x = x_ref[d].astype(F32)[rows:]
        lags = jnp.concatenate(
            [tap_ref[d * per : (d + 1) * per, :], cot_ref[d * per : (d + 1) * per, :]], axis=0
        )
        low = lags - lags.astype(BF16).astype(F32)
        out_ref[d] = jnp.concatenate([state, lags, low], axis=0).astype(BF16)
        state = decay * state + x
        total = total + x * front_ref[d].astype(F32)[:rows]
    sum_ref[...] = total


def collect_kernel(size, x_ref, sum_ref, lam_ref, out_ref):
    rows, modes = sum_ref.shape[0], lam_ref.shape[0]
    lags = jnp.sum(x_ref[...].astype(F32), axis=0)[rows:]
    lags = lags[:2] + lags[2:]
    lam = jnp.concatenate([lam_ref[...], jnp.zeros((LANES - modes, LANES), F32)], axis=0)
    second = exact_dot(jnp.broadcast_to(lags[1:2], (8, LANES)), lam, NT)[:1]
    lane, place = iota((LANES, LANES), 0), iota((LANES, LANES), 1)
    for q in range(rows):
        pick = (place == modes + lane // size * rows + q).astype(F32)
        second = second + exact_dot(jnp.broadcast_to(sum_ref[q : q + 1, :], (8, LANES)), pick, NN)[:1]
    message = jnp.concatenate([lags[:1], second], axis=0)
    out_ref[...] = jnp.broadcast_to(message[None], out_ref.shape)


def finish_kernel(scale, per, rows, x_ref, norm_ref, res_ref, tap_ref):
    modes, count = norm_ref.shape
    x = x_ref[:count]
    for k in range(count, x_ref.shape[0], count):
        x = x + x_ref[k : k + count]
    tap_ref[...] = x[:, 0, :] * scale
    rest = x[:, 1, :]
    total = rest
    h, j = iota(rest.shape, 0) % per, iota(rest.shape, 1) // rows
    for delta in range(1 - per, per):
        moved = rest if delta == 0 else pltpu.roll(rest, delta % count, 0)
        moved = pltpu.roll(moved, (-modes - rows * delta) % LANES, 1)
        total = total + jnp.where(h - j == delta, moved, 0.0)
    res_ref[...] = total.T[:modes] * norm_ref[...] * scale


def call(body, width, step, chunk, specs, outs, args, micros, room=60):
    kinds = list(specs) + [rows for rows, kind in outs]
    chunks = step // chunk

    def kernel(*refs):
        def part(c, carry):
            views = []
            for ref, rows in zip(refs, kinds):
                if rows is None:
                    views.append(ref.at[:, pl.ds(pl.multiple_of(c * chunk, chunk), chunk)])
                else:
                    views.append(ref.at[pl.ds(pl.multiple_of(c * rows, rows), rows), :])
            body(*views)
            return carry

        lax.fori_loop(0, chunks, part, 0)

    def block(rows):
        if rows is None:
            return pl.BlockSpec((LANES, step), lambda i: (0, i))
        return pl.BlockSpec((rows * chunks, LANES), lambda i: (i, 0))

    def shape(rows, kind):
        if rows is None:
            return jax.ShapeDtypeStruct((LANES, width), kind)
        return jax.ShapeDtypeStruct((rows * (width // chunk), LANES), kind)

    nbytes = sum(a.size * a.dtype.itemsize for a in args)
    return pl.pallas_call(
        kernel,
        grid=(width // step,),
        in_specs=[block(rows) for rows in specs],
        out_specs=[block(rows) for rows, kind in outs],
        out_shape=[shape(rows, kind) for rows, kind in outs],
        compiler_params=pltpu.CompilerParams(vmem_limit_bytes=room * 1024 * 1024),
        cost_estimate=pl.CostEstimate(flops=micros * 1_000_000_000, bytes_accessed=nbytes, transcendentals=0),
    )(*args)


def whole(body, outs, args, room=8):
    return pl.pallas_call(
        body,
        out_shape=[jax.ShapeDtypeStruct(shape, kind) for shape, kind in outs],
        compiler_params=pltpu.CompilerParams(vmem_limit_bytes=room * 1024 * 1024),
        cost_estimate=pl.CostEstimate(flops=2_000_000_000, bytes_accessed=1 << 20, transcendentals=0),
    )(*args)


def shifted(x, by):
    count = lax.axis_size("ctx")
    return lax.ppermute(x, "ctx", [(i, i + by) for i in range(count) if 0 <= i + by < count])


def exchange(x, axes="ctx"):
    return lax.all_to_all(x, axes, split_axis=0, concat_axis=0, tiled=True)


def on_device(inputs, gate_li, gate_mr, cotangent, residues, rates, taps):
    seq, gate, cot = inputs[0], gate_li[0], cotangent[0]
    width = seq.shape[1]
    groups, modes = rates.shape
    size = width // groups
    per = LANES // size
    tiles = width // LANES
    reps, count = lax.axis_size("rep"), lax.axis_size("ctx")
    me = lax.axis_index("ctx")
    own_rows = tiles * modes // count
    step = chunk = min(2048, width)
    state_rows = chunk // LANES * modes
    table_rows = per * state_rows
    group_rows = chunk // size
    carry_rows, tile_rows = chunk, chunk // LANES

    scaled = (cot.astype(F32) * gate_mr[0].astype(F32)).astype(BF16)
    after = shifted(scaled, -1)

    norm = jnp.sqrt(-jnp.expm1(-2.0 * rates))
    weight = residues * norm
    rate_rows = jnp.broadcast_to(rates.reshape(-1, 1), (groups * modes, LANES))
    rate_row = rates.reshape(tiles, per * modes)
    rate_row = jnp.concatenate([rate_row, rate_row], axis=1)
    weight_row = weight.reshape(tiles, per * modes)
    weight_row = jnp.concatenate([weight_row, weight_row], axis=1)
    decay, lam_own = pl.pallas_call(
        functools.partial(owner_kernel, size, own_rows),
        in_specs=[pl.BlockSpec(memory_space=pltpu.SMEM), pl.BlockSpec(memory_space=pltpu.VMEM)],
        out_shape=[
            jax.ShapeDtypeStruct((own_rows, LANES), F32), jax.ShapeDtypeStruct((modes, LANES), F32)
        ],
        compiler_params=pltpu.CompilerParams(vmem_limit_bytes=8 * 1024 * 1024),
        cost_estimate=pl.CostEstimate(flops=1_000_000_000, bytes_accessed=1 << 16, transcendentals=0),
    )(me.astype(jnp.int32).reshape(1, 1), rates)
    bind = functools.partial
    states = call(
        bind(states_kernel, size, modes), width, step, chunk, [None, table_rows], [(state_rows, BF16)],
        [seq, rate_rows], 3,
    )[0]
    ends = exchange(states.reshape(count, own_rows, LANES))

    after, decay, lam_own = lax.optimization_barrier((after, decay, lam_own))
    grad_mixer, back_states = call(
        bind(mixer_back_kernel, size, modes), width, step, chunk,
        [None, None, None, group_rows, table_rows], [(None, F32), (state_rows, F32)],
        [scaled, after, gate, taps, rate_rows], 8,
    )
    first = whole(
        scan_kernel, [((count, 2 * own_rows, LANES), BF16)],
        [ends, decay, back_states.reshape(count, own_rows, LANES)],
    )[0]
    second = exchange(first)
    late = lax.optimization_barrier((rates.T, weight.T, taps, first))[:3]
    filt, filt_back, taps_back = whole(filters_kernel, [(taps.shape, F32)] * 3, late, 60)
    local, front_table, lag_cot = call(
        bind(local_kernel, size), width, step, chunk,
        [None, None, None, group_rows, tile_rows, tile_rows],
        [(None, F32), (carry_rows, BF16), (group_rows, F32)],
        [seq, gate, grad_mixer, filt_back, rate_row, weight_row], 10,
    )
    mixer_in, lag_taps = call(
        bind(values_kernel, size, modes), width, step, chunk,
        [None, None, None, None, carry_rows, 2 * state_rows], [(None, BF16), (group_rows, F32)],
        [local, gate, scaled, after, front_table, second.reshape(-1, LANES)], 6,
    )
    before = shifted(mixer_in, 1)
    message, state_sums = whole(
        back_scan_kernel, [(first.shape, BF16), (decay.shape, F32)],
        [second, decay, first, lag_taps, lag_cot], 60,
    )
    third = exchange(message)
    grad_gate_mr = call(
        bind(mixer_kernel, size), width, step, chunk, [None, None, group_rows, None], [(None, BF16)],
        [mixer_in, before, taps_back, cot], 7, 32,
    )[0]
    third, grad_gate_mr = lax.optimization_barrier((third, grad_gate_mr))
    spread = whole(
        bind(collect_kernel, size), [((reps * count, 2, LANES), F32)], [third, state_sums, lam_own]
    )[0]
    got = exchange(spread, ("rep", "ctx"))
    local = lax.optimization_barrier((local, spread))[0]
    grad_gate_li = call(
        bind(gate_grad_kernel, size, modes), width, step, chunk,
        [None, None, carry_rows, 2 * state_rows], [(None, BF16)],
        [local, grad_mixer, front_table, second.reshape(-1, LANES)], 4,
    )[0]
    grad_inputs = call(
        bind(input_grad_kernel, size, modes), width, step, chunk,
        [None, None, group_rows, tile_rows, tile_rows, 2 * state_rows], [(None, BF16)],
        [grad_mixer, gate, filt, rate_row, weight_row, third.reshape(-1, LANES)], 7,
    )[0]
    grad_residues, grad_taps = whole(
        bind(finish_kernel, 1.0 / math.sqrt(reps * count * LANES), per, own_rows),
        [((modes, groups), F32), (taps.shape, F32)], [got, norm.T],
    )
    return grad_inputs[None], grad_gate_li[None], grad_gate_mr[None], grad_residues.T, grad_taps


def solution(mesh):
    big = P("rep", "ctx", None)
    return jax.shard_map(
        on_device,
        mesh=mesh,
        in_specs=(big, big, big, big, P(), P(), P()),
        out_specs=(big, big, big, P(), P()),
        check_vma=False,
    )
```

```python
import functools
import math

import jax
import jax.numpy as jnp
from jax import lax
from jax.experimental import pallas as pl
from jax.experimental.pallas import tpu as pltpu
from jax.sharding import PartitionSpec as P

F32 = jnp.float32
BF16 = jnp.bfloat16
LANES = 128
NN = (((1,), (0,)), ((), ()))
NT = (((1,), (1,)), ((), ()))
TN = (((0,), (0,)), ((), ()))


def dot(left, right, dims=NN):
    return lax.dot_general(left, right, dims, preferred_element_type=F32)


def split(x):
    high = x.astype(BF16)
    return high, (x - high.astype(F32)).astype(BF16)


def iota(shape, dim):
    return lax.broadcasted_iota(jnp.int32, shape, dim)


def roll_left(x, amount):
    return pltpu.roll(x, x.shape[1] - amount, 1)


def pick_groups(stacked, rows, size):
    lane_group = iota((rows, LANES), 1) // size
    out = stacked[:rows]
    for g in range(1, LANES // size):
        out = jnp.where(lane_group == g, stacked[g * rows : (g + 1) * rows], out)
    return out


def spread_groups(x, size):
    lane_group = iota(x.shape, 1) // size
    zero = jnp.zeros_like(x)
    return jnp.concatenate(
        [jnp.where(lane_group == g, x, zero) for g in range(LANES // size)], axis=0
    )


def circulant(row):
    return split(pltpu.roll(jnp.broadcast_to(row, (LANES, LANES)), 0, 1, stride=1, stride_axis=0))


def masked(row, keeps):
    parts = circulant(row)
    zero = jnp.zeros_like(parts[0])
    return jnp.concatenate([jnp.where(keep, part, zero) for part in parts for keep in keeps], axis=1)


def toeplitz(rows_ref, i, per, keeps):
    return jnp.concatenate(
        [masked(rows_ref[i * per + g : i * per + g + 1, :], keeps) for g in range(per)], axis=0
    )


def lag_rows(z):
    sums = [None] * 4
    for k in range(LANES // 8):
        part = z[8 * k : 8 * k + 8]
        part = roll_left(part, 8 * k) if k else part
        sums[k % 4] = part if sums[k % 4] is None else sums[k % 4] + part
    return (sums[0] + sums[1]) + (sums[2] + sums[3])


def lag_sums(rows):
    rows = jnp.concatenate(rows, axis=0)
    sub = iota(rows.shape, 0)
    for bit in (4, 2, 1):
        rows = jnp.where((sub & bit) != 0, roll_left(rows, bit), rows)
    return jnp.sum(rows.reshape(-1, 8, LANES), axis=1)


def carry_table(rate_ref, weight_ref, i, steps):
    high, low = split(weight_ref[i : i + 1, :] * jnp.exp(-rate_ref[i : i + 1, :] * steps))
    return jnp.where(iota(steps.shape, 1) < LANES // 2, high, low)


def carried_part(table, ref, i, modes, size):
    x = ref[i * 2 * modes : (i + 1) * 2 * modes, :].astype(F32)
    x = jnp.concatenate([x[k : k + 4] for k in range(0, 2 * modes, 8)], axis=0)
    x = spread_groups(x, size).astype(BF16)
    return dot(table, jnp.concatenate([x, x], axis=0))


def mode_sums(table, x, size, modes):
    high, low = split(table)
    if x.dtype == BF16:
        prod = dot(jnp.concatenate([high, low], axis=0), x)
    else:
        left = jnp.concatenate(
            [jnp.concatenate([high, high], axis=1), jnp.concatenate([low, low], axis=1)], axis=0
        )
        prod = dot(left, jnp.concatenate(split(x), axis=0))
    half = prod.shape[0] // 2
    return pick_groups(prod[:half] + prod[half:], modes, size)


def tiles_of(ref):
    return [slice(i * LANES, (i + 1) * LANES) for i in range(ref.shape[1] // LANES)]


def states_kernel(size, modes, x_ref, rate_ref, out_ref):
    rows = LANES // size * modes
    steps = LANES - 1.0 - iota((rows, LANES), 1).astype(F32)
    out = [
        mode_sums(jnp.exp(-rate_ref[i * rows : (i + 1) * rows, :] * steps), x_ref[:, lanes], size, modes)
        for i, lanes in enumerate(tiles_of(x_ref))
    ]
    out_ref[...] = jnp.concatenate(out, axis=0).astype(out_ref.dtype)


def mixer_back_kernel(size, modes, own_ref, next_ref, gate_ref, taps_ref, rate_ref, gm_ref, out_ref):
    per = LANES // size
    rows = per * modes
    row, col = iota((LANES, LANES), 0), iota((LANES, LANES), 1)
    tiles = tiles_of(own_ref)
    cots, out = [], []
    for i, lanes in enumerate(tiles):
        own, after = own_ref[:, lanes], next_ref[:, lanes]
        left = toeplitz(taps_ref, i, per, [col >= row, col < row])
        prod = dot(left, jnp.concatenate([own, after, own, after], axis=0))
        grad_mixer = pick_groups(prod, LANES, size)
        gm_ref[:, lanes] = grad_mixer
        cots.append(grad_mixer * gate_ref[:, lanes].astype(F32))
    steps = iota((rows, LANES), 1).astype(F32) + 1.0
    for i, lanes in enumerate(tiles):
        table = jnp.exp(-rate_ref[i * rows : (i + 1) * rows, :] * steps)
        out.append(mode_sums(table, cots[i], size, modes))
    out_ref[...] = jnp.concatenate(out, axis=0)


def local_kernel(
    size, x_ref, gate_ref, gm_ref, filt_ref, rate_ref, weight_ref, out_ref, table_ref, lag_ref
):
    per = LANES // size
    row, col = iota((LANES, LANES), 0), iota((LANES, LANES), 1)
    up = row.astype(F32)
    tiles = tiles_of(x_ref)
    lag_parts = []
    for i, lanes in enumerate(tiles):
        x = x_ref[:, lanes]
        prod = dot(toeplitz(filt_ref, i, per, [col <= row]), jnp.concatenate([x, x], axis=0))
        out_ref[:, lanes] = pick_groups(prod, LANES, size)
    for i in range(len(tiles)):
        table_ref[i * LANES : (i + 1) * LANES, :] = carry_table(rate_ref, weight_ref, i, up + 1.0)
    for i, lanes in enumerate(tiles):
        cot = (gm_ref[:, lanes] * gate_ref[:, lanes].astype(F32)).astype(BF16)
        pairs = dot(spread_groups(x_ref[:, lanes], size), cot, NT)
        for g in range(per):
            lag_parts.append(lag_rows(jnp.where(col >= row, pairs[g * LANES : (g + 1) * LANES], 0.0)))
    lag_ref[...] = lag_sums(lag_parts)


def values_kernel(
    size, modes, local_ref, gate_ref, own_ref, next_ref, table_ref, enter_ref, mix_ref, lag_ref
):
    per = LANES // size
    row, col = iota((LANES, LANES), 0), iota((LANES, LANES), 1)
    tiles = tiles_of(local_ref)
    mixes, lag_parts = [], []
    for i, lanes in enumerate(tiles):
        table = table_ref[i * LANES : (i + 1) * LANES, :]
        full = local_ref[:, lanes] + carried_part(table, enter_ref, i, modes, size)
        mixes.append((gate_ref[:, lanes].astype(F32) * full).astype(BF16))
    for i, lanes in enumerate(tiles):
        mix_ref[:, lanes] = mixes[i]
        both = jnp.concatenate([own_ref[:, lanes], next_ref[:, lanes]], axis=0)
        pairs = dot(spread_groups(mixes[i], size), both, NT)
        for g in range(per):
            z = pairs[g * LANES : (g + 1) * LANES]
            lag_parts.append(lag_rows(jnp.where(col >= row, z[:, :LANES], z[:, LANES:])))
    lag_ref[...] = lag_sums(lag_parts)


def gate_grad_kernel(size, modes, local_ref, gm_ref, table_ref, enter_ref, out_ref):
    for i, lanes in enumerate(tiles_of(local_ref)):
        table = table_ref[i * LANES : (i + 1) * LANES, :]
        full = local_ref[:, lanes] + carried_part(table, enter_ref, i, modes, size)
        out_ref[:, lanes] = (gm_ref[:, lanes] * full).astype(BF16)


def input_grad_kernel(
    size, modes, gm_ref, gate_ref, filt_ref, rate_ref, weight_ref, enter_ref, out_ref
):
    per = LANES // size
    row, col = iota((LANES, LANES), 0), iota((LANES, LANES), 1)
    for i, lanes in enumerate(tiles_of(gm_ref)):
        left = toeplitz(filt_ref, i, per, [col >= row])
        high, low = split(gm_ref[:, lanes] * gate_ref[:, lanes].astype(F32))
        prod = dot(
            jnp.concatenate([left, left[:, :LANES]], axis=1), jnp.concatenate([high, high, low], axis=0)
        )
        table = carry_table(rate_ref, weight_ref, i, LANES - 1.0 - row.astype(F32))
        carried = carried_part(table, enter_ref, i, modes, size)
        out_ref[:, lanes] = (pick_groups(prod, LANES, size) + carried).astype(BF16)


def mixer_kernel(size, own_ref, before_ref, taps_ref, cot_ref, out_ref):
    per = LANES // size
    row, col = iota((LANES, LANES), 0), iota((LANES, LANES), 1)
    for i, lanes in enumerate(tiles_of(own_ref)):
        own, before = own_ref[:, lanes], before_ref[:, lanes]
        left = toeplitz(taps_ref, i, per, [col <= row, col > row])
        prod = dot(left, jnp.concatenate([own, before, own, before], axis=0))
        mixed = pick_groups(prod, LANES, size)
        out_ref[:, lanes] = (cot_ref[:, lanes].astype(F32) * mixed).astype(BF16)


def exact_dot(left, right, dims=NN):
    return lax.dot_general(
        left, right, dims, precision=lax.Precision.HIGHEST, preferred_element_type=F32
    )


def filters_kernel(rates_ref, weight_ref, taps_ref, filt_ref, filt_back_ref, taps_back_ref):
    rates, weight, taps = rates_ref[...].T, weight_ref[...].T, taps_ref[...]
    groups, modes = rates.shape
    lag = iota((groups, LANES), 1).astype(F32)
    filt = jnp.zeros((groups, LANES), F32)
    for m in range(modes):
        filt = filt + weight[:, m : m + 1] * jnp.exp(-rates[:, m : m + 1] * lag)
    mirror = ((iota((LANES, LANES), 0) + iota((LANES, LANES), 1)) % LANES == 0).astype(F32)
    filt_ref[...] = filt
    filt_back_ref[...] = exact_dot(filt, mirror)
    taps_back_ref[...] = exact_dot(taps, mirror)


def owner_kernel(size, own_rows, me_ref, rates_ref, decay_ref, lam_ref):
    me = me_ref[0, 0]
    rates = rates_ref[...]
    groups, modes = rates.shape
    per, parts = LANES // size, modes // own_rows
    pick = iota((8, modes), 1) == me % parts * own_rows + iota((8, modes), 0)
    chosen = exact_dot(pick.astype(F32), rates, NT)
    spread = iota((groups, LANES), 0) == me // parts * per + iota((groups, LANES), 1) // size
    decay_ref[...] = jnp.exp(-exact_dot(chosen, spread.astype(F32))[:own_rows] * LANES)
    own = (iota((groups, LANES), 0) == me).astype(F32)
    lam_ref[...] = jnp.exp(-exact_dot(rates, own, TN) * iota((modes, LANES), 1).astype(F32))


def scan_kernel(x_ref, decay_ref, beside_ref, out_ref):
    decay = decay_ref[...]
    state = jnp.zeros_like(decay)
    for d in range(x_ref.shape[0]):
        out_ref[d] = jnp.concatenate([state, beside_ref[d]], axis=0).astype(BF16)
        state = decay * state + x_ref[d].astype(F32)


def back_scan_kernel(x_ref, decay_ref, front_ref, tap_ref, cot_ref, out_ref, sum_ref):
    decay = decay_ref[...]
    rows = decay.shape[0]
    per = tap_ref.shape[0] // x_ref.shape[0]
    state = jnp.zeros_like(decay)
    total = jnp.zeros_like(decay)
    for d in reversed(range(x_ref.shape[0])):
        x = x_ref[d].astype(F32)[rows:]
        lags = jnp.concatenate(
            [tap_ref[d * per : (d + 1) * per, :], cot_ref[d * per : (d + 1) * per, :]], axis=0
        )
        low = lags - lags.astype(BF16).astype(F32)
        out_ref[d] = jnp.concatenate([state, lags, low], axis=0).astype(BF16)
        state = decay * state + x
        total = total + x * front_ref[d].astype(F32)[:rows]
    sum_ref[...] = total


def collect_kernel(size, x_ref, sum_ref, lam_ref, out_ref):
    rows, modes = sum_ref.shape[0], lam_ref.shape[0]
    lags = jnp.sum(x_ref[...].astype(F32), axis=0)[rows:]
    lags = lags[:2] + lags[2:]
    lam = jnp.concatenate([lam_ref[...], jnp.zeros((LANES - modes, LANES), F32)], axis=0)
    second = exact_dot(jnp.broadcast_to(lags[1:2], (8, LANES)), lam, NT)[:1]
    lane, place = iota((LANES, LANES), 0), iota((LANES, LANES), 1)
    for q in range(rows):
        pick = (place == modes + lane // size * rows + q).astype(F32)
        second = second + exact_dot(jnp.broadcast_to(sum_ref[q : q + 1, :], (8, LANES)), pick, NN)[:1]
    message = jnp.concatenate([lags[:1], second], axis=0)
    out_ref[...] = jnp.broadcast_to(message[None], out_ref.shape)


def finish_kernel(scale, per, rows, x_ref, norm_ref, res_ref, tap_ref):
    modes, count = norm_ref.shape
    x = x_ref[:count]
    for k in range(count, x_ref.shape[0], count):
        x = x + x_ref[k : k + count]
    tap_ref[...] = x[:, 0, :] * scale
    rest = x[:, 1, :]
    total = rest
    h, j = iota(rest.shape, 0) % per, iota(rest.shape, 1) // rows
    for delta in range(1 - per, per):
        moved = rest if delta == 0 else pltpu.roll(rest, delta % count, 0)
        moved = pltpu.roll(moved, (-modes - rows * delta) % LANES, 1)
        total = total + jnp.where(h - j == delta, moved, 0.0)
    res_ref[...] = total.T[:modes] * norm_ref[...] * scale


def call(body, width, step, chunk, specs, outs, args, micros, room=60):
    kinds = list(specs) + [rows for rows, kind in outs]
    chunks = step // chunk

    def kernel(*refs):
        def part(c, carry):
            views = []
            for ref, rows in zip(refs, kinds):
                if rows is None:
                    views.append(ref.at[:, pl.ds(pl.multiple_of(c * chunk, chunk), chunk)])
                else:
                    views.append(ref.at[pl.ds(pl.multiple_of(c * rows, rows), rows), :])
            body(*views)
            return carry

        lax.fori_loop(0, chunks, part, 0)

    def block(rows):
        if rows is None:
            return pl.BlockSpec((LANES, step), lambda i: (0, i))
        return pl.BlockSpec((rows * chunks, LANES), lambda i: (i, 0))

    def shape(rows, kind):
        if rows is None:
            return jax.ShapeDtypeStruct((LANES, width), kind)
        return jax.ShapeDtypeStruct((rows * (width // chunk), LANES), kind)

    nbytes = sum(a.size * a.dtype.itemsize for a in args)
    return pl.pallas_call(
        kernel,
        grid=(width // step,),
        in_specs=[block(rows) for rows in specs],
        out_specs=[block(rows) for rows, kind in outs],
        out_shape=[shape(rows, kind) for rows, kind in outs],
        compiler_params=pltpu.CompilerParams(vmem_limit_bytes=room * 1024 * 1024),
        cost_estimate=pl.CostEstimate(flops=micros * 1_000_000_000, bytes_accessed=nbytes, transcendentals=0),
    )(*args)


def whole(body, outs, args, room=8):
    return pl.pallas_call(
        body,
        out_shape=[jax.ShapeDtypeStruct(shape, kind) for shape, kind in outs],
        compiler_params=pltpu.CompilerParams(vmem_limit_bytes=room * 1024 * 1024),
        cost_estimate=pl.CostEstimate(flops=2_000_000_000, bytes_accessed=1 << 20, transcendentals=0),
    )(*args)


def shifted(x, by):
    count = lax.axis_size("ctx")
    return lax.ppermute(x, "ctx", [(i, i + by) for i in range(count) if 0 <= i + by < count])


def exchange(x, axes="ctx"):
    return lax.all_to_all(x, axes, split_axis=0, concat_axis=0, tiled=True)


def on_device(inputs, gate_li, gate_mr, cotangent, residues, rates, taps):
    seq, gate, cot = inputs[0], gate_li[0], cotangent[0]
    width = seq.shape[1]
    groups, modes = rates.shape
    size = width // groups
    per = LANES // size
    tiles = width // LANES
    reps, count = lax.axis_size("rep"), lax.axis_size("ctx")
    me = lax.axis_index("ctx")
    own_rows = tiles * modes // count
    step = chunk = min(2048, width)
    state_rows = chunk // LANES * modes
    table_rows = per * state_rows
    group_rows = chunk // size
    carry_rows, tile_rows = chunk, chunk // LANES

    scaled = (cot.astype(F32) * gate_mr[0].astype(F32)).astype(BF16)
    after = shifted(scaled, -1)

    norm = jnp.sqrt(-jnp.expm1(-2.0 * rates))
    weight = residues * norm
    rate_rows = jnp.broadcast_to(rates.reshape(-1, 1), (groups * modes, LANES))
    rate_row = rates.reshape(tiles, per * modes)
    rate_row = jnp.concatenate([rate_row, rate_row], axis=1)
    weight_row = weight.reshape(tiles, per * modes)
    weight_row = jnp.concatenate([weight_row, weight_row], axis=1)
    decay, lam_own = pl.pallas_call(
        functools.partial(owner_kernel, size, own_rows),
        in_specs=[pl.BlockSpec(memory_space=pltpu.SMEM), pl.BlockSpec(memory_space=pltpu.VMEM)],
        out_shape=[
            jax.ShapeDtypeStruct((own_rows, LANES), F32), jax.ShapeDtypeStruct((modes, LANES), F32)
        ],
        compiler_params=pltpu.CompilerParams(vmem_limit_bytes=8 * 1024 * 1024),
        cost_estimate=pl.CostEstimate(flops=1_000_000_000, bytes_accessed=1 << 16, transcendentals=0),
    )(me.astype(jnp.int32).reshape(1, 1), rates)
    bind = functools.partial
    states = call(
        bind(states_kernel, size, modes), width, step, chunk, [None, table_rows], [(state_rows, BF16)],
        [seq, rate_rows], 3,
    )[0]
    ends = exchange(states.reshape(count, own_rows, LANES))

    after, decay, lam_own = lax.optimization_barrier((after, decay, lam_own))
    grad_mixer, back_states = call(
        bind(mixer_back_kernel, size, modes), width, step, chunk,
        [None, None, None, group_rows, table_rows], [(None, F32), (state_rows, F32)],
        [scaled, after, gate, taps, rate_rows], 8, 52,
    )
    first = whole(
        scan_kernel, [((count, 2 * own_rows, LANES), BF16)],
        [ends, decay, back_states.reshape(count, own_rows, LANES)],
    )[0]
    second = exchange(first)
    late = lax.optimization_barrier((rates.T, weight.T, taps, first))[:3]
    filt, filt_back, taps_back = whole(filters_kernel, [(taps.shape, F32)] * 3, late, 60)
    local, front_table, lag_cot = call(
        bind(local_kernel, size), width, step, chunk,
        [None, None, None, group_rows, tile_rows, tile_rows],
        [(None, F32), (carry_rows, BF16), (group_rows, F32)],
        [seq, gate, grad_mixer, filt_back, rate_row, weight_row], 10,
    )
    mixer_in, lag_taps = call(
        bind(values_kernel, size, modes), width, step, chunk,
        [None, None, None, None, carry_rows, 2 * state_rows], [(None, BF16), (group_rows, F32)],
        [local, gate, scaled, after, front_table, second.reshape(-1, LANES)], 6,
    )
    before = shifted(mixer_in, 1)
    message, state_sums = whole(
        back_scan_kernel, [(first.shape, BF16), (decay.shape, F32)],
        [second, decay, first, lag_taps, lag_cot], 60,
    )
    third = exchange(message)
    grad_gate_mr = call(
        bind(mixer_kernel, size), width, step, chunk, [None, None, group_rows, None], [(None, BF16)],
        [mixer_in, before, taps_back, cot], 7, 32,
    )[0]
    third, grad_gate_mr = lax.optimization_barrier((third, grad_gate_mr))
    spread = whole(
        bind(collect_kernel, size), [((reps * count, 2, LANES), F32)], [third, state_sums, lam_own]
    )[0]
    got = exchange(spread, ("rep", "ctx"))
    local = lax.optimization_barrier((local, spread))[0]
    grad_gate_li = call(
        bind(gate_grad_kernel, size, modes), width, step, chunk,
        [None, None, carry_rows, 2 * state_rows], [(None, BF16)],
        [local, grad_mixer, front_table, second.reshape(-1, LANES)], 4,
    )[0]
    grad_inputs = call(
        bind(input_grad_kernel, size, modes), width, step, chunk,
        [None, None, group_rows, tile_rows, tile_rows, 2 * state_rows], [(None, BF16)],
        [grad_mixer, gate, filt, rate_row, weight_row, third.reshape(-1, LANES)], 7,
    )[0]
    grad_residues, grad_taps = whole(
        bind(finish_kernel, 1.0 / math.sqrt(reps * count * LANES), per, own_rows),
        [((modes, groups), F32), (taps.shape, F32)], [got, norm.T],
    )
    return grad_inputs[None], grad_gate_li[None], grad_gate_mr[None], grad_residues.T, grad_taps


def solution(mesh):
    big = P("rep", "ctx", None)
    return jax.shard_map(
        on_device,
        mesh=mesh,
        in_specs=(big, big, big, big, P(), P(), P()),
        out_specs=(big, big, big, P(), P()),
        check_vma=False,
    )
```

```python
import functools
import math

import jax
import jax.numpy as jnp
from jax import lax
from jax.experimental import pallas as pl
from jax.experimental.pallas import tpu as pltpu
from jax.sharding import PartitionSpec as P

F32 = jnp.float32
BF16 = jnp.bfloat16
LANES = 128
NN = (((1,), (0,)), ((), ()))
NT = (((1,), (1,)), ((), ()))
TN = (((0,), (0,)), ((), ()))


def dot(left, right, dims=NN):
    return lax.dot_general(left, right, dims, preferred_element_type=F32)


def split(x):
    high = x.astype(BF16)
    return high, (x - high.astype(F32)).astype(BF16)


def iota(shape, dim):
    return lax.broadcasted_iota(jnp.int32, shape, dim)


def roll_left(x, amount):
    return pltpu.roll(x, x.shape[1] - amount, 1)


def pick_groups(stacked, rows, size):
    lane_group = iota((rows, LANES), 1) // size
    out = stacked[:rows]
    for g in range(1, LANES // size):
        out = jnp.where(lane_group == g, stacked[g * rows : (g + 1) * rows], out)
    return out


def spread_groups(x, size):
    lane_group = iota(x.shape, 1) // size
    zero = jnp.zeros_like(x)
    return jnp.concatenate(
        [jnp.where(lane_group == g, x, zero) for g in range(LANES // size)], axis=0
    )


def circulant(row):
    return split(pltpu.roll(jnp.broadcast_to(row, (LANES, LANES)), 0, 1, stride=1, stride_axis=0))


def masked(row, keeps):
    parts = circulant(row)
    zero = jnp.zeros_like(parts[0])
    return jnp.concatenate([jnp.where(keep, part, zero) for part in parts for keep in keeps], axis=1)


def toeplitz(rows_ref, i, per, keeps):
    return jnp.concatenate(
        [masked(rows_ref[i * per + g : i * per + g + 1, :], keeps) for g in range(per)], axis=0
    )


def lag_rows(z):
    sums = [None] * 4
    for k in range(LANES // 8):
        part = z[8 * k : 8 * k + 8]
        part = roll_left(part, 8 * k) if k else part
        sums[k % 4] = part if sums[k % 4] is None else sums[k % 4] + part
    return (sums[0] + sums[1]) + (sums[2] + sums[3])


def lag_sums(rows):
    rows = jnp.concatenate(rows, axis=0)
    sub = iota(rows.shape, 0)
    for bit in (4, 2, 1):
        rows = jnp.where((sub & bit) != 0, roll_left(rows, bit), rows)
    return jnp.sum(rows.reshape(-1, 8, LANES), axis=1)


def carry_table(rate_ref, weight_ref, i, steps):
    high, low = split(weight_ref[i : i + 1, :] * jnp.exp(-rate_ref[i : i + 1, :] * steps))
    return jnp.where(iota(steps.shape, 1) < LANES // 2, high, low)


def carried_part(table, ref, i, modes, size):
    x = ref[i * 2 * modes : (i + 1) * 2 * modes, :].astype(F32)
    x = jnp.concatenate([x[k : k + 4] for k in range(0, 2 * modes, 8)], axis=0)
    x = spread_groups(x, size).astype(BF16)
    return dot(table, jnp.concatenate([x, x], axis=0))


def mode_sums(table, x, size, modes):
    high, low = split(table)
    if x.dtype == BF16:
        prod = dot(jnp.concatenate([high, low], axis=0), x)
    else:
        left = jnp.concatenate(
            [jnp.concatenate([high, high], axis=1), jnp.concatenate([low, low], axis=1)], axis=0
        )
        prod = dot(left, jnp.concatenate(split(x), axis=0))
    half = prod.shape[0] // 2
    return pick_groups(prod[:half] + prod[half:], modes, size)


def tiles_of(ref):
    return [slice(i * LANES, (i + 1) * LANES) for i in range(ref.shape[1] // LANES)]


def states_kernel(size, modes, x_ref, rate_ref, out_ref):
    rows = LANES // size * modes
    steps = LANES - 1.0 - iota((rows, LANES), 1).astype(F32)
    out = [
        mode_sums(jnp.exp(-rate_ref[i * rows : (i + 1) * rows, :] * steps), x_ref[:, lanes], size, modes)
        for i, lanes in enumerate(tiles_of(x_ref))
    ]
    out_ref[...] = jnp.concatenate(out, axis=0).astype(out_ref.dtype)


def mixer_back_kernel(size, modes, own_ref, next_ref, gate_ref, taps_ref, rate_ref, gm_ref, out_ref):
    per = LANES // size
    rows = per * modes
    row, col = iota((LANES, LANES), 0), iota((LANES, LANES), 1)
    tiles = tiles_of(own_ref)
    cots, out = [], []
    for i, lanes in enumerate(tiles):
        own, after = own_ref[:, lanes], next_ref[:, lanes]
        left = toeplitz(taps_ref, i, per, [col >= row, col < row])
        prod = dot(left, jnp.concatenate([own, after, own, after], axis=0))
        grad_mixer = pick_groups(prod, LANES, size)
        gm_ref[:, lanes] = grad_mixer
        cots.append(grad_mixer * gate_ref[:, lanes].astype(F32))
    steps = iota((rows, LANES), 1).astype(F32) + 1.0
    for i, lanes in enumerate(tiles):
        table = jnp.exp(-rate_ref[i * rows : (i + 1) * rows, :] * steps)
        out.append(mode_sums(table, cots[i], size, modes))
    out_ref[...] = jnp.concatenate(out, axis=0)


def local_kernel(
    size, x_ref, gate_ref, gm_ref, filt_ref, rate_ref, weight_ref, out_ref, table_ref, lag_ref
):
    per = LANES // size
    row, col = iota((LANES, LANES), 0), iota((LANES, LANES), 1)
    up = row.astype(F32)
    tiles = tiles_of(x_ref)
    lag_parts = []
    for i, lanes in enumerate(tiles):
        x = x_ref[:, lanes]
        prod = dot(toeplitz(filt_ref, i, per, [col <= row]), jnp.concatenate([x, x], axis=0))
        out_ref[:, lanes] = pick_groups(prod, LANES, size)
    for i in range(len(tiles)):
        table_ref[i * LANES : (i + 1) * LANES, :] = carry_table(rate_ref, weight_ref, i, up + 1.0)
    for i, lanes in enumerate(tiles):
        cot = (gm_ref[:, lanes] * gate_ref[:, lanes].astype(F32)).astype(BF16)
        pairs = dot(spread_groups(x_ref[:, lanes], size), cot, NT)
        for g in range(per):
            lag_parts.append(lag_rows(jnp.where(col >= row, pairs[g * LANES : (g + 1) * LANES], 0.0)))
    lag_ref[...] = lag_sums(lag_parts)


def values_kernel(
    size, modes, local_ref, gate_ref, own_ref, next_ref, table_ref, enter_ref, mix_ref, lag_ref
):
    per = LANES // size
    row, col = iota((LANES, LANES), 0), iota((LANES, LANES), 1)
    tiles = tiles_of(local_ref)
    mixes, lag_parts = [], []
    for i, lanes in enumerate(tiles):
        table = table_ref[i * LANES : (i + 1) * LANES, :]
        full = local_ref[:, lanes] + carried_part(table, enter_ref, i, modes, size)
        mixes.append((gate_ref[:, lanes].astype(F32) * full).astype(BF16))
    for i, lanes in enumerate(tiles):
        mix_ref[:, lanes] = mixes[i]
        both = jnp.concatenate([own_ref[:, lanes], next_ref[:, lanes]], axis=0)
        pairs = dot(spread_groups(mixes[i], size), both, NT)
        for g in range(per):
            z = pairs[g * LANES : (g + 1) * LANES]
            lag_parts.append(lag_rows(jnp.where(col >= row, z[:, :LANES], z[:, LANES:])))
    lag_ref[...] = lag_sums(lag_parts)


def gate_grad_kernel(size, modes, local_ref, gm_ref, table_ref, enter_ref, out_ref):
    for i, lanes in enumerate(tiles_of(local_ref)):
        table = table_ref[i * LANES : (i + 1) * LANES, :]
        full = local_ref[:, lanes] + carried_part(table, enter_ref, i, modes, size)
        out_ref[:, lanes] = (gm_ref[:, lanes] * full).astype(BF16)


def input_grad_kernel(
    size, modes, gm_ref, gate_ref, filt_ref, rate_ref, weight_ref, enter_ref, out_ref
):
    per = LANES // size
    row, col = iota((LANES, LANES), 0), iota((LANES, LANES), 1)
    for i, lanes in enumerate(tiles_of(gm_ref)):
        left = toeplitz(filt_ref, i, per, [col >= row])
        high, low = split(gm_ref[:, lanes] * gate_ref[:, lanes].astype(F32))
        prod = dot(
            jnp.concatenate([left, left[:, :LANES]], axis=1), jnp.concatenate([high, high, low], axis=0)
        )
        table = carry_table(rate_ref, weight_ref, i, LANES - 1.0 - row.astype(F32))
        carried = carried_part(table, enter_ref, i, modes, size)
        out_ref[:, lanes] = (pick_groups(prod, LANES, size) + carried).astype(BF16)


def mixer_kernel(size, own_ref, before_ref, taps_ref, cot_ref, out_ref):
    per = LANES // size
    row, col = iota((LANES, LANES), 0), iota((LANES, LANES), 1)
    for i, lanes in enumerate(tiles_of(own_ref)):
        own, before = own_ref[:, lanes], before_ref[:, lanes]
        left = toeplitz(taps_ref, i, per, [col <= row, col > row])
        prod = dot(left, jnp.concatenate([own, before, own, before], axis=0))
        mixed = pick_groups(prod, LANES, size)
        out_ref[:, lanes] = (cot_ref[:, lanes].astype(F32) * mixed).astype(BF16)


def exact_dot(left, right, dims=NN):
    return lax.dot_general(
        left, right, dims, precision=lax.Precision.HIGHEST, preferred_element_type=F32
    )


def filters_kernel(rates_ref, weight_ref, taps_ref, filt_ref, filt_back_ref, taps_back_ref):
    rates, weight, taps = rates_ref[...].T, weight_ref[...].T, taps_ref[...]
    groups, modes = rates.shape
    lag = iota((groups, LANES), 1).astype(F32)
    filt = jnp.zeros((groups, LANES), F32)
    for m in range(modes):
        filt = filt + weight[:, m : m + 1] * jnp.exp(-rates[:, m : m + 1] * lag)
    mirror = ((iota((LANES, LANES), 0) + iota((LANES, LANES), 1)) % LANES == 0).astype(F32)
    filt_ref[...] = filt
    filt_back_ref[...] = exact_dot(filt, mirror)
    taps_back_ref[...] = exact_dot(taps, mirror)


def owner_kernel(size, own_rows, me_ref, rates_ref, decay_ref, lam_ref):
    me = me_ref[0, 0]
    rates = rates_ref[...]
    groups, modes = rates.shape
    per, parts = LANES // size, modes // own_rows
    pick = iota((8, modes), 1) == me % parts * own_rows + iota((8, modes), 0)
    chosen = exact_dot(pick.astype(F32), rates, NT)
    spread = iota((groups, LANES), 0) == me // parts * per + iota((groups, LANES), 1) // size
    decay_ref[...] = jnp.exp(-exact_dot(chosen, spread.astype(F32))[:own_rows] * LANES)
    own = (iota((groups, LANES), 0) == me).astype(F32)
    lam_ref[...] = jnp.exp(-exact_dot(rates, own, TN) * iota((modes, LANES), 1).astype(F32))


def scan_kernel(x_ref, decay_ref, beside_ref, out_ref):
    decay = decay_ref[...]
    state = jnp.zeros_like(decay)
    for d in range(x_ref.shape[0]):
        out_ref[d] = jnp.concatenate([state, beside_ref[d]], axis=0).astype(BF16)
        state = decay * state + x_ref[d].astype(F32)


def back_scan_kernel(x_ref, decay_ref, front_ref, tap_ref, cot_ref, out_ref, sum_ref):
    decay = decay_ref[...]
    rows = decay.shape[0]
    per = tap_ref.shape[0] // x_ref.shape[0]
    state = jnp.zeros_like(decay)
    total = jnp.zeros_like(decay)
    for d in reversed(range(x_ref.shape[0])):
        x = x_ref[d].astype(F32)[rows:]
        lags = jnp.concatenate(
            [tap_ref[d * per : (d + 1) * per, :], cot_ref[d * per : (d + 1) * per, :]], axis=0
        )
        low = lags - lags.astype(BF16).astype(F32)
        out_ref[d] = jnp.concatenate([state, lags, low], axis=0).astype(BF16)
        state = decay * state + x
        total = total + x * front_ref[d].astype(F32)[:rows]
    sum_ref[...] = total


def collect_kernel(size, x_ref, sum_ref, lam_ref, out_ref):
    rows, modes = sum_ref.shape[0], lam_ref.shape[0]
    lags = jnp.sum(x_ref[...].astype(F32), axis=0)[rows:]
    lags = lags[:2] + lags[2:]
    lam = jnp.concatenate([lam_ref[...], jnp.zeros((LANES - modes, LANES), F32)], axis=0)
    second = exact_dot(jnp.broadcast_to(lags[1:2], (8, LANES)), lam, NT)[:1]
    lane, place = iota((LANES, LANES), 0), iota((LANES, LANES), 1)
    for q in range(rows):
        pick = (place == modes + lane // size * rows + q).astype(F32)
        second = second + exact_dot(jnp.broadcast_to(sum_ref[q : q + 1, :], (8, LANES)), pick, NN)[:1]
    message = jnp.concatenate([lags[:1], second], axis=0)
    out_ref[...] = jnp.broadcast_to(message[None], out_ref.shape)


def finish_kernel(scale, per, rows, x_ref, norm_ref, res_ref, tap_ref):
    modes, count = norm_ref.shape
    x = x_ref[:count]
    for k in range(count, x_ref.shape[0], count):
        x = x + x_ref[k : k + count]
    tap_ref[...] = x[:, 0, :] * scale
    rest = x[:, 1, :]
    total = rest
    h, j = iota(rest.shape, 0) % per, iota(rest.shape, 1) // rows
    for delta in range(1 - per, per):
        moved = rest if delta == 0 else pltpu.roll(rest, delta % count, 0)
        moved = pltpu.roll(moved, (-modes - rows * delta) % LANES, 1)
        total = total + jnp.where(h - j == delta, moved, 0.0)
    res_ref[...] = total.T[:modes] * norm_ref[...] * scale


def call(body, width, step, chunk, specs, outs, args, micros, room=60):
    kinds = list(specs) + [rows for rows, kind in outs]
    chunks = step // chunk

    def kernel(*refs):
        def part(c, carry):
            views = []
            for ref, rows in zip(refs, kinds):
                if rows is None:
                    views.append(ref.at[:, pl.ds(pl.multiple_of(c * chunk, chunk), chunk)])
                else:
                    views.append(ref.at[pl.ds(pl.multiple_of(c * rows, rows), rows), :])
            body(*views)
            return carry

        lax.fori_loop(0, chunks, part, 0)

    def block(rows):
        if rows is None:
            return pl.BlockSpec((LANES, step), lambda i: (0, i))
        return pl.BlockSpec((rows * chunks, LANES), lambda i: (i, 0))

    def shape(rows, kind):
        if rows is None:
            return jax.ShapeDtypeStruct((LANES, width), kind)
        return jax.ShapeDtypeStruct((rows * (width // chunk), LANES), kind)

    nbytes = sum(a.size * a.dtype.itemsize for a in args)
    return pl.pallas_call(
        kernel,
        grid=(width // step,),
        in_specs=[block(rows) for rows in specs],
        out_specs=[block(rows) for rows, kind in outs],
        out_shape=[shape(rows, kind) for rows, kind in outs],
        compiler_params=pltpu.CompilerParams(vmem_limit_bytes=room * 1024 * 1024),
        cost_estimate=pl.CostEstimate(flops=micros * 1_000_000_000, bytes_accessed=nbytes, transcendentals=0),
    )(*args)


def whole(body, outs, args, room=8):
    return pl.pallas_call(
        body,
        out_shape=[jax.ShapeDtypeStruct(shape, kind) for shape, kind in outs],
        compiler_params=pltpu.CompilerParams(vmem_limit_bytes=room * 1024 * 1024),
        cost_estimate=pl.CostEstimate(flops=2_000_000_000, bytes_accessed=1 << 20, transcendentals=0),
    )(*args)


def shifted(x, by):
    count = lax.axis_size("ctx")
    return lax.ppermute(x, "ctx", [(i, i + by) for i in range(count) if 0 <= i + by < count])


def exchange(x, axes="ctx"):
    return lax.all_to_all(x, axes, split_axis=0, concat_axis=0, tiled=True)


def on_device(inputs, gate_li, gate_mr, cotangent, residues, rates, taps):
    seq, gate, cot = inputs[0], gate_li[0], cotangent[0]
    width = seq.shape[1]
    groups, modes = rates.shape
    size = width // groups
    per = LANES // size
    tiles = width // LANES
    reps, count = lax.axis_size("rep"), lax.axis_size("ctx")
    me = lax.axis_index("ctx")
    own_rows = tiles * modes // count
    step = chunk = min(2048, width)
    state_rows = chunk // LANES * modes
    table_rows = per * state_rows
    group_rows = chunk // size
    carry_rows, tile_rows = chunk, chunk // LANES

    scaled = (cot.astype(F32) * gate_mr[0].astype(F32)).astype(BF16)
    after = shifted(scaled, -1)

    norm = jnp.sqrt(-jnp.expm1(-2.0 * rates))
    weight = residues * norm
    rate_rows = jnp.broadcast_to(rates.reshape(-1, 1), (groups * modes, LANES))
    rate_row = rates.reshape(tiles, per * modes)
    rate_row = jnp.concatenate([rate_row, rate_row], axis=1)
    weight_row = weight.reshape(tiles, per * modes)
    weight_row = jnp.concatenate([weight_row, weight_row], axis=1)
    decay, lam_own = pl.pallas_call(
        functools.partial(owner_kernel, size, own_rows),
        in_specs=[pl.BlockSpec(memory_space=pltpu.SMEM), pl.BlockSpec(memory_space=pltpu.VMEM)],
        out_shape=[
            jax.ShapeDtypeStruct((own_rows, LANES), F32), jax.ShapeDtypeStruct((modes, LANES), F32)
        ],
        compiler_params=pltpu.CompilerParams(vmem_limit_bytes=8 * 1024 * 1024),
        cost_estimate=pl.CostEstimate(flops=1_000_000_000, bytes_accessed=1 << 16, transcendentals=0),
    )(me.astype(jnp.int32).reshape(1, 1), rates)
    bind = functools.partial
    states = call(
        bind(states_kernel, size, modes), width, step, chunk, [None, table_rows], [(state_rows, BF16)],
        [seq, rate_rows], 3,
    )[0]
    ends = exchange(states.reshape(count, own_rows, LANES))

    after, decay, lam_own = lax.optimization_barrier((after, decay, lam_own))
    grad_mixer, back_states = call(
        bind(mixer_back_kernel, size, modes), width, step, chunk,
        [None, None, None, group_rows, table_rows], [(None, F32), (state_rows, F32)],
        [scaled, after, gate, taps, rate_rows], 8, 52,
    )
    first = whole(
        scan_kernel, [((count, 2 * own_rows, LANES), BF16)],
        [ends, decay, back_states.reshape(count, own_rows, LANES)],
    )[0]
    second = exchange(first)
    late = lax.optimization_barrier((rates.T, weight.T, taps, first))[:3]
    filt, filt_back, taps_back = whole(filters_kernel, [(taps.shape, F32)] * 3, late, 60)
    local, front_table, lag_cot = call(
        bind(local_kernel, size), width, step, chunk,
        [None, None, None, group_rows, tile_rows, tile_rows],
        [(None, F32), (carry_rows, BF16), (group_rows, F32)],
        [seq, gate, grad_mixer, filt_back, rate_row, weight_row], 10,
    )
    mixer_in, lag_taps = call(
        bind(values_kernel, size, modes), width, step, chunk,
        [None, None, None, None, carry_rows, 2 * state_rows], [(None, BF16), (group_rows, F32)],
        [local, gate, scaled, after, front_table, second.reshape(-1, LANES)], 6, 52,
    )
    before = shifted(mixer_in, 1)
    message, state_sums = whole(
        back_scan_kernel, [(first.shape, BF16), (decay.shape, F32)],
        [second, decay, first, lag_taps, lag_cot], 52,
    )
    third = exchange(message)
    grad_gate_mr = call(
        bind(mixer_kernel, size), width, step, chunk, [None, None, group_rows, None], [(None, BF16)],
        [mixer_in, before, taps_back, cot], 7, 32,
    )[0]
    third, grad_gate_mr = lax.optimization_barrier((third, grad_gate_mr))
    spread = whole(
        bind(collect_kernel, size), [((reps * count, 2, LANES), F32)], [third, state_sums, lam_own]
    )[0]
    got = exchange(spread, ("rep", "ctx"))
    local = lax.optimization_barrier((local, spread))[0]
    grad_gate_li = call(
        bind(gate_grad_kernel, size, modes), width, step, chunk,
        [None, None, carry_rows, 2 * state_rows], [(None, BF16)],
        [local, grad_mixer, front_table, second.reshape(-1, LANES)], 4,
    )[0]
    grad_inputs = call(
        bind(input_grad_kernel, size, modes), width, step, chunk,
        [None, None, group_rows, tile_rows, tile_rows, 2 * state_rows], [(None, BF16)],
        [grad_mixer, gate, filt, rate_row, weight_row, third.reshape(-1, LANES)], 7,
    )[0]
    grad_residues, grad_taps = whole(
        bind(finish_kernel, 1.0 / math.sqrt(reps * count * LANES), per, own_rows),
        [((modes, groups), F32), (taps.shape, F32)], [got, norm.T],
    )
    return grad_inputs[None], grad_gate_li[None], grad_gate_mr[None], grad_residues.T, grad_taps


def solution(mesh):
    big = P("rep", "ctx", None)
    return jax.shard_map(
        on_device,
        mesh=mesh,
        in_specs=(big, big, big, big, P(), P(), P()),
        out_specs=(big, big, big, P(), P()),
        check_vma=False,
    )
```
